32 devices in a mesh: beam: 2 (over y), chan: 16 (over z, x, core).
Axes of the slice: x: 2, y: 2, z: 4, core: 2. Of those that a mesh axis runs over, the one named last changes fastest.
Arguments:
- filterbank: bfloat16 [2048, 4096], P(('beam', 'chan')), parts along dimension 0
- shift_table: int32 [511], replicated, may hold values from 0 to 511, as said below
- box_widths: int32 [8], replicated, may hold values from 1 to 255, as said below
Outputs:
- dedispersed: bfloat16 [512, 4096], P(('beam', 'chan')), parts along dimension 0
- peaks: float32 [16, 256], P('beam', 'chan'), parts along dimension 0
The draws below stay inside these ranges and needn't reach their ends.
There are 2 independent parts, one for each index of `beam`. The reference program is written for one: setup_inputs(seed, part) draws one part's arguments, and reference() takes and returns one part's arrays. A program takes and returns all parts, laid end to end along the dimension named above; an argument that names none is the same for every part. Nothing has to cross between parts.
Inputs may be any that keep to these rules, and one draw needn't show every extreme that they name: `shift_table`: entry k - 1 + j, for k a power of two up to 256 and j < k, is the delay for merged trial j of a section with k trials; it equals 2 j or 2 j + 1. `box_widths`: entry i lies between 2**i and 2**(i+1) - 1.
All inputs are finite; a program needn't handle non-finite values.
Results may differ from the reference program's by a relative error of at most 0.001.
Values sent between devices are 32-bit elements; how exact they have to be, the bound alone decides.
A program may use at most 64 MiB of HBM per device.

```python
import math
import jax
import jax.numpy as jnp
from jax import lax

CH_DEV = 64
ROWS = 16
TIME = 4096
WIDTHS = 8
CHANNELS = 1024
TRIALS = 256
CROSS = 4
N_CHAN = 16


def draw_filterbank(key, part):
    subkeys = jax.random.split(key, 4)
    chan_scale = jnp.exp(jax.random.uniform(subkeys[0], (CHANNELS, 1), jnp.float32, 0.0, math.log(10.0)))
    offset = jax.random.uniform(subkeys[1], (CHANNELS, 1), jnp.float32, -5.0, 5.0)
    time_scale = jnp.exp(jax.random.uniform(subkeys[2], (1, TIME), jnp.float32, 0.0, math.log(10.0)))
    fluctuation = jax.random.normal(subkeys[3], (CHANNELS, TIME), jnp.float32)
    values = offset + chan_scale * fluctuation * time_scale
    return values.astype(jnp.bfloat16)


def draw_shift_table(key, part):
    entries = 2 * TRIALS - 1
    position = jnp.arange(entries, dtype=jnp.int32) + 1
    section_size = jnp.ones((entries,), jnp.int32)
    for exponent in range(1, 31):
        section_size = jnp.where(position >= 2 ** exponent, 2 ** exponent, section_size)
    within = position - section_size
    parity = jax.random.randint(key, (entries,), 0, 2, dtype=jnp.int32)
    parity = jnp.where(within == 0, jnp.minimum(section_size - 1, 1), parity)
    parity = jnp.where(position == entries, 1, parity)
    return 2 * within + parity


def draw_box_widths(key, part):
    exponent = jnp.arange(WIDTHS, dtype=jnp.int32)
    lowest = jnp.left_shift(jnp.ones((WIDTHS,), jnp.int32), exponent)
    jitter = jax.random.randint(key, (WIDTHS,), 0, 2 ** 30, dtype=jnp.int32) % lowest
    widths_out = lowest + jitter
    return jnp.where(exponent == WIDTHS - 1, 2 * lowest - 1, widths_out)


def setup_inputs(seed: int = 0, part: int = 0) -> dict:
    splits = jax.random.split(jax.random.key(seed), 4)
    part_keys = jax.random.split(jax.random.fold_in(splits[3], part), 4)
    filterbank = draw_filterbank(jax.random.fold_in(jax.random.fold_in(splits[3], part), 71), part)
    shift_table = draw_shift_table(jax.random.fold_in(splits[3], 71), part)
    box_widths = draw_box_widths(jax.random.fold_in(splits[3], 71), part)
    return dict(filterbank=filterbank, shift_table=shift_table, box_widths=box_widths)


epsilon = 1e-05

def advance(rows_in, shifts):
    length = rows_in.shape[-1]
    padded = jnp.concatenate([rows_in, jnp.zeros_like(rows_in)], axis=-1)

    def single(strip, amount):
        return lax.dynamic_slice_in_dim(strip, jnp.minimum(amount, length), length, strip.ndim - 1)
    return jax.vmap(single, in_axes=(-2, 0), out_axes=-2)(padded, shifts)

def merge_pairs(subbands, shift_table, trials_now):
    paired = subbands.reshape(subbands.shape[0] // 2, 2, subbands.shape[1], subbands.shape[2])
    lower_rows = paired[:, 0]
    upper_rows = paired[:, 1]
    if trials_now > subbands.shape[1]:
        lower_rows = jnp.repeat(lower_rows, 2, axis=1)
        upper_rows = jnp.repeat(upper_rows, 2, axis=1)
    return lower_rows + advance(upper_rows, shift_table[trials_now - 1:2 * trials_now - 1])

def local_tree(spectra, shift_table):
    chan_count = spectra.shape[0]
    subbands = spectra[:, None, :]
    band_span = 1
    while band_span < chan_count:
        band_span *= 2
        subbands = merge_pairs(subbands, shift_table, max(1, band_span * ROWS // chan_count))
    return subbands[0]

def normalize(channel_block):
    values = channel_block.astype(jnp.float32)
    centre = lax.optimization_barrier(jnp.mean(values, axis=1, keepdims=True))
    spread = lax.optimization_barrier(jnp.mean(jnp.square(values - centre), axis=1, keepdims=True))
    return (values - centre) * lax.rsqrt(spread + epsilon)

def boxcar_peaks(scaled, box_widths):
    length = scaled.shape[1]
    running = jnp.cumsum(scaled, axis=1)
    padded = jnp.concatenate([jnp.zeros_like(running), running], axis=1)

    def single(box_width):
        earlier = lax.dynamic_slice_in_dim(padded, length - box_width, length, 1)
        box_sums = (running - earlier) * lax.rsqrt(box_width.astype(jnp.float32))
        return lax.optimization_barrier(jnp.max(box_sums, axis=1))
    return lax.map(single, box_widths)

def reference(filterbank, shift_table, box_widths):
    groups = filterbank.reshape(N_CHAN, CH_DEV, TIME)

    def add_group(summed, channel_block):
        return (summed + lax.optimization_barrier(jnp.sum(normalize(channel_block), axis=0)), None)
    summed, _ = lax.scan(add_group, jnp.zeros((TIME,), jnp.float32), groups)
    channel_mean = summed / CHANNELS

    def local_part(channel_block):
        return local_tree(normalize(channel_block) - channel_mean, shift_table)
    subbands = lax.map(local_part, groups)
    while subbands.shape[0] > 1:
        subbands = merge_pairs(subbands, shift_table, 2 * subbands.shape[1])
    series = subbands[0]
    block_index = jnp.arange(N_CHAN, dtype=jnp.int32)
    reversed_block = jnp.zeros((N_CHAN,), jnp.int32)
    for bit_number in range(CROSS):
        reversed_block = reversed_block + (block_index >> bit_number & 1) * 2 ** (CROSS - 1 - bit_number)
    ordered = series.reshape(N_CHAN, ROWS, TIME)[reversed_block].reshape(TRIALS, TIME)
    centre = lax.optimization_barrier(jnp.mean(ordered, axis=1, keepdims=True))
    spread = lax.optimization_barrier(jnp.mean(jnp.square(ordered - centre), axis=1, keepdims=True))
    scaled = (ordered - centre) * lax.rsqrt(spread + epsilon)
    dedispersed = scaled.astype(jnp.bfloat16)
    peaks = boxcar_peaks(scaled, box_widths)
    return (dedispersed, peaks)
```

```python
import functools

import jax
import jax.numpy as jnp
from jax import lax
from jax.experimental import pallas as pl
from jax.experimental.pallas import tpu as pltpu
from jax.sharding import PartitionSpec as P

ROWS = 16
SUB = 8
LANES = 128
GROUP_BITS = 4

epsilon = 1e-05

VMEM_LIMIT = 48 * 1024 * 1024


def lane_index():
    return lax.broadcasted_iota(jnp.int32, (SUB, LANES), 1)


def next_sublane(tile):
    sub = lax.broadcasted_iota(jnp.int32, tile.shape, tile.ndim - 2)
    return jnp.where(sub == SUB - 1, 0.0, pltpu.roll(tile, SUB - 1, tile.ndim - 2))


def combine(tiles, amount):
    back = (LANES - amount) & (LANES - 1)
    turned = [pltpu.roll(tile, back, tile.ndim - 1) for tile in tiles]
    lane = lax.broadcasted_iota(jnp.int32, tiles[0].shape, tiles[0].ndim - 1)
    keep = lane < LANES - amount
    return [jnp.where(keep, turned[i], turned[i + 1]) for i in range(len(tiles) - 1)]


def advanced(tiles, amount):
    return combine(list(tiles) + [next_sublane(tiles[0])], amount)


def plus(first, second):
    return [a + b for a, b in zip(first, second)]


def digit_bits(digit, bits):
    return [(digit // (1 << i)) % 2 for i in range(bits)]


def partner(bit_values, k):
    flipped = [1 - b if k >> i & 1 else b for i, b in enumerate(bit_values)]
    plain = sum((b * (1 << i) for i, b in enumerate(flipped)), 0)
    turned = sum((b * (1 << len(flipped) - 1 - i) for i, b in enumerate(flipped)), 0)
    return plain, turned


def peer_rounds(bits):
    return sorted(range(1, 1 << bits), reverse=True)


def enter(peers):
    barrier = pltpu.get_barrier_semaphore()
    for peer in peers:
        pl.semaphore_signal(
            barrier, inc=1, device_id={"chan": peer}, device_id_type=pl.DeviceIdType.MESH
        )
    return barrier


def remote(src, dst, send_sem, recv_sem, k, peer):
    return pltpu.make_async_remote_copy(
        src_ref=src,
        dst_ref=dst,
        send_sem=send_sem.at[k],
        recv_sem=recv_sem.at[k],
        device_id={"chan": peer},
        device_id_type=pl.DeviceIdType.MESH,
    )


def front_kernel(
    bits, total_channels, fb, table, rows, mean_row,
    norm, base, level2, level4, level8, send, pieces, landed, gathered,
    scat_send, scat_recv, gath_send, gath_recv, row_send, row_recv, own_sem,
):
    group = 1 << bits
    held = ROWS // group
    channels, length = fb.shape
    wide = length // SUB
    count = wide // LANES
    me = lax.axis_index("chan")
    digit = me % group
    mine = digit_bits(digit, bits)
    _, my_turn = partner(mine, 0)
    rounds = peer_rounds(bits)
    peers = {}
    for k in rounds:
        plain, turned = partner(mine, k)
        peers[k] = (me - digit + plain, plain, turned)
    barrier = enter([peers[k][0] for k in rounds])

    step = 16
    for first in range(0, channels, step):
        values = fb[first : first + step, :].astype(jnp.float32)
        centre = jnp.mean(values, axis=1, keepdims=True)
        moved = values - centre
        spread = jnp.mean(jnp.square(moved), axis=1, keepdims=True)
        scaled = moved * lax.rsqrt(spread + epsilon)
        for s in range(SUB):
            for m in range(count):
                at = s * wide + m * LANES
                norm[m, pl.ds(first * SUB + s, step, stride=SUB), :] = scaled[:, at : at + LANES]

    single = table[0]

    def four(q, partial):
        row = []
        for c in range(4):
            at = pl.multiple_of((4 * q + c) * SUB, SUB)
            row.append([norm[m, pl.ds(at, SUB), :] for m in range(count)])
        summed = plus(plus(row[0], row[1]), plus(row[2], row[3]))
        low = plus(row[0], advanced(row[1], single))
        high = plus(row[2], advanced(row[3], single))
        merged = plus(low, advanced(high, single))
        for m in range(count):
            base[q, :, m * LANES : (m + 1) * LANES] = merged[m]
        return tuple(plus(partial, summed))

    partial = lax.fori_loop(
        0, channels // 4, four, tuple(jnp.zeros((SUB, LANES), jnp.float32) for _ in range(count)), unroll=2
    )
    for e in range(ROWS):
        s, m = 2 * (e // count), e % count
        pieces[e] = partial[m][s : s + 2, :]

    if rounds:
        pl.semaphore_wait(barrier, len(rounds))
    scatter = {}
    for k in rounds:
        chan, plain, turned = peers[k]
        scatter[k] = remote(
            pieces.at[pl.ds(plain * held, held)], landed.at[digit], scat_send, scat_recv, k, chan
        )
        scatter[k].start()

    def tiles_of(load):
        return [load(slice(m * LANES, (m + 1) * LANES)) for m in range(count)]

    subs = channels // 4
    view = base.reshape(subs // 2, 2, 1, SUB, wide)
    trials = 1
    for target in (level2, level4, level8, send):
        trials *= 2
        subs //= 2
        for i in range(trials):
            low = tiles_of(lambda w: view[:, 0, i // 2, :, w])
            high = tiles_of(lambda w: view[:, 1, i // 2, :, w])
            merged = plus(low, advanced(high, table[trials - 1 + i]))
            for m in range(count):
                w = slice(m * LANES, (m + 1) * LANES)
                if subs > 1:
                    target[:, i, :, w] = merged[m]
                else:
                    target[i, :, w] = merged[m][0]
        if subs > 1:
            view = target.reshape(subs // 2, 2, trials, SUB, wide)

    copies = {}
    for k in rounds:
        chan, plain, turned = peers[k]
        copies[k] = remote(
            send.at[pl.ds(turned * held, held)], rows.at[pl.ds(digit * held, held)], row_send, row_recv, k, chan
        )
        copies[k].start()
    own = pltpu.make_async_copy(
        send.at[pl.ds(my_turn * held, held)], rows.at[pl.ds(digit * held, held)], own_sem
    )
    own.start()

    total = pieces[pl.ds(digit * held, held)]
    for k in rounds:
        scatter[k].wait_recv()
        total = total + landed[peers[k][1]]
    gathered[pl.ds(digit * held, held)] = total * (1.0 / total_channels)
    gather = {}
    for k in rounds:
        here = gathered.at[pl.ds(digit * held, held)]
        gather[k] = remote(here, here, gath_send, gath_recv, k, peers[k][0])
        gather[k].start()
    for k in rounds:
        gather[k].wait_recv()
    mean = []
    for m in range(count):
        mean.append(jnp.concatenate([gathered[a * count + m] for a in range(SUB // 2)], axis=0))

    for j in range(held):
        trial = my_turn * held + j
        line = plus(mean, advanced(mean, single))
        line = plus(line, advanced(line, single))
        for level in range(1, 5):
            now = trial // (1 << 4 - level)
            line = plus(line, advanced(line, table[(1 << level) - 1 + now]))
        for m in range(count):
            mean_row[j, :, m * LANES : (m + 1) * LANES] = line[m]

    own.wait()
    for k in rounds:
        copies[k].wait_recv()
    for k in rounds:
        scatter[k].wait_send()
        gather[k].wait_send()
        copies[k].wait_send()


def front(filterbank, shift_table, bits, total_channels):
    channels, length = filterbank.shape
    wide = length // SUB
    group = 1 << bits
    held = ROWS // group
    f32 = jnp.float32
    return pl.pallas_call(
        functools.partial(front_kernel, bits, total_channels),
        out_shape=(
            jax.ShapeDtypeStruct((ROWS, SUB, wide), f32),
            jax.ShapeDtypeStruct((held, SUB, wide), f32),
        ),
        in_specs=[pl.BlockSpec(memory_space=pltpu.VMEM), pl.BlockSpec(memory_space=pltpu.SMEM)],
        out_specs=(pl.BlockSpec(memory_space=pl.ANY), pl.BlockSpec(memory_space=pltpu.VMEM)),
        scratch_shapes=[
            pltpu.VMEM((wide // LANES, channels * SUB, LANES), f32),
            pltpu.VMEM((16, SUB, wide), f32),
            pltpu.VMEM((8, 2, SUB, wide), f32),
            pltpu.VMEM((4, 4, SUB, wide), f32),
            pltpu.VMEM((2, 8, SUB, wide), f32),
            pltpu.VMEM((ROWS, SUB, wide), f32),
            pltpu.VMEM((ROWS, 2, LANES), f32),
            pltpu.VMEM((group, held, 2, LANES), f32),
            pltpu.VMEM((ROWS, 2, LANES), f32),
        ]
        + [pltpu.SemaphoreType.DMA((group,))] * 6
        + [pltpu.SemaphoreType.DMA],
        compiler_params=pltpu.CompilerParams(
            collective_id=0, has_side_effects=True, vmem_limit_bytes=VMEM_LIMIT
        ),
    )(filterbank, shift_table)


def exchange_kernel(bits, stride, block, rows, row_send, row_recv, own_sem):
    group = 1 << bits
    held = ROWS // group
    me = lax.axis_index("chan")
    digit = (me // stride) % group
    mine = digit_bits(digit, bits)
    _, my_turn = partner(mine, 0)
    rounds = peer_rounds(bits)
    peers = {}
    for k in rounds:
        plain, turned = partner(mine, k)
        peers[k] = (me + (plain - digit) * stride, turned)
    barrier = enter([peers[k][0] for k in rounds])
    pl.semaphore_wait(barrier, len(rounds))
    there = rows.at[pl.ds(digit * held, held)]
    copies = {}
    for k in rounds:
        chan, turned = peers[k]
        copies[k] = remote(block.at[pl.ds(turned * held, held)], there, row_send, row_recv, k, chan)
        copies[k].start()
    own = pltpu.make_async_copy(block.at[pl.ds(my_turn * held, held)], there, own_sem)
    own.start()
    own.wait()
    for k in rounds:
        copies[k].wait()


def exchange(block, bits, stride, number):
    group = 1 << bits
    return pl.pallas_call(
        functools.partial(exchange_kernel, bits, stride),
        out_shape=jax.ShapeDtypeStruct(block.shape, block.dtype),
        in_specs=[pl.BlockSpec(memory_space=pltpu.VMEM)],
        out_specs=pl.BlockSpec(memory_space=pl.ANY),
        scratch_shapes=[pltpu.SemaphoreType.DMA((group,))] * 2 + [pltpu.SemaphoreType.DMA],
        compiler_params=pltpu.CompilerParams(
            collective_id=number, has_side_effects=True, vmem_limit_bytes=VMEM_LIMIT
        ),
    )(block)


def merge_rows(bits, merged, largest, block, correction, table, position, levels):
    group = 1 << bits
    held = ROWS // group
    wide = block.shape[-1]
    count = wide // LANES
    sub = lax.broadcasted_iota(jnp.int32, (SUB, LANES), 0)

    def put(level, row, tiles, is_upper):
        for m in range(count):
            levels[level, row, :, m * LANES : (m + 1) * LANES] = tiles[m]
            if is_upper:
                levels[level, row, :, wide + m * LANES : wide + (m + 1) * LANES] = next_sublane(tiles[m])

    for row in range(ROWS):
        tiles = []
        for m in range(count):
            w = slice(m * LANES, (m + 1) * LANES)
            tile = block[row, :, w]
            tiles.append(tile if correction is None else tile - correction[row % held, :, w])
        put(0, row, tiles, row // held % 2 == 1)
    place = position[0]
    trials = held
    for level in range(bits):
        now = 2 * trials
        whole = merged * ROWS << level + 1
        for i in range(now):
            shift = table[whole - 1 + place * now + i]
            within = shift & (wide - 1)
            at = within // LANES
            for q in range(ROWS // now):
                low = 2 * q * trials + i // 2
                high = low + trials
                tiles = [
                    levels[level, high, :, pl.ds(pl.multiple_of((at + m) * LANES, LANES), LANES)]
                    for m in range(count + 1)
                ]
                moved = combine(tiles, within & (LANES - 1))
                if largest >= wide:
                    up = jnp.minimum(shift // wide, SUB)
                    moved = [
                        jnp.where(sub < SUB - up, pltpu.roll(tile, (SUB - up) & (SUB - 1), 0), 0.0)
                        for tile in moved
                    ]
                lower = [levels[level, low, :, m * LANES : (m + 1) * LANES] for m in range(count)]
                put(level + 1, q * now + i, plus(lower, moved), level + 1 < bits and q % 2 == 1)
        trials = now


def middle_kernel(bits, merged, largest, corrected, position, table, block, *rest):
    correction = rest[0] if corrected else None
    out, levels = rest[-2:]
    merge_rows(bits, merged, largest, block, correction, table, position, levels)
    for row in range(ROWS):
        out[row] = levels[bits, row, :, : block.shape[-1]]


def back_kernel(bits, merged, largest, corrected, position, table, widths, block, *rest):
    correction = rest[0] if corrected else None
    dedispersed, peaks, levels, flat = rest[-4:]
    wide = block.shape[-1]
    length = wide * SUB
    merge_rows(bits, merged, largest, block, correction, table, position, levels)
    for row in range(ROWS):
        for m in range(wide // LANES):
            flat[m, row * SUB : (row + 1) * SUB, :] = levels[bits, row, :, m * LANES : (m + 1) * LANES]
    series = [
        jnp.concatenate([flat[m, pl.ds(s, ROWS, stride=SUB), :] for m in range(wide // LANES)], axis=1)
        for s in range(SUB)
    ]
    summed = series[0]
    for part in series[1:]:
        summed = summed + part
    centre = jnp.sum(summed, axis=1, keepdims=True) * (1.0 / length)
    series = [part - centre for part in series]
    squared = jnp.square(series[0])
    for part in series[1:]:
        squared = squared + jnp.square(part)
    spread = jnp.sum(squared, axis=1, keepdims=True) * (1.0 / length)
    factor = lax.rsqrt(spread + epsilon)
    series = [part * factor for part in series]
    for s in range(SUB):
        dedispersed[:, s * wide : (s + 1) * wide] = series[s].astype(jnp.bfloat16)

    piece = 2 * LANES
    stacked = jnp.concatenate(
        [part[:, a : a + piece] for part in series for a in range(0, wide, piece)], axis=0
    )
    triangle = jnp.where(
        lax.broadcasted_iota(jnp.int32, (piece, piece), 0) <= lax.broadcasted_iota(jnp.int32, (piece, piece), 1),
        1.0,
        0.0,
    ).astype(jnp.bfloat16)
    rest_value = stacked
    inner = None
    for _ in range(3):
        top = rest_value.astype(jnp.bfloat16)
        rest_value = rest_value - top.astype(jnp.float32)
        product = jnp.dot(top, triangle, preferred_element_type=jnp.float32)
        inner = product if inner is None else inner + product
    offset = jnp.zeros((ROWS, 1), jnp.float32)
    prefix = []
    for p in range(length // piece):
        one = inner[p * ROWS : (p + 1) * ROWS, :] + offset
        offset = one[:, piece - 1 : piece]
        prefix += [one[:, :LANES], one[:, LANES:]]

    lane = lax.broadcasted_iota(jnp.int32, (ROWS, LANES), 1)
    diagonal = lane == lax.broadcasted_iota(jnp.int32, (ROWS, LANES), 0)
    zero = jnp.zeros((ROWS, LANES), jnp.float32)
    count = peaks.shape[0]
    for i in range(count):
        width = widths[i]
        whole, amount = divmod(1 << i, LANES)
        amount = width - whole * LANES
        keep = lane >= amount
        best = None
        before = zero
        for c in range(len(prefix)):
            source = c - whole
            now = pltpu.roll(prefix[source], amount, 1) if source >= 0 else zero
            box = prefix[c] - jnp.where(keep, now, before)
            before = now
            best = box if best is None else jnp.maximum(best, box)
        root = lax.rsqrt(jnp.full((ROWS, 1), width, jnp.int32).astype(jnp.float32))
        column = jnp.max(best, axis=1, keepdims=True) * root
        line = jnp.sum(jnp.where(diagonal, column, 0.0), axis=0, keepdims=True)
        peaks[i : i + 1, :] = line[:, :ROWS]


def merge(block, correction, shift_table, position, bits, merged, box_widths):
    wide = block.shape[-1]
    largest = 2 * ((merged * ROWS << bits) - 1) + 1
    corrected = correction is not None
    smem = pl.BlockSpec(memory_space=pltpu.SMEM)
    vmem = pl.BlockSpec(memory_space=pltpu.VMEM)
    levels = pltpu.VMEM((bits + 1, ROWS, SUB, 2 * wide), jnp.float32)
    params = pltpu.CompilerParams(vmem_limit_bytes=VMEM_LIMIT)
    data = (block, correction) if corrected else (block,)
    if box_widths is None:
        return pl.pallas_call(
            functools.partial(middle_kernel, bits, merged, largest, corrected),
            out_shape=jax.ShapeDtypeStruct(block.shape, jnp.float32),
            in_specs=[smem] * 2 + [vmem] * len(data),
            out_specs=vmem,
            scratch_shapes=[levels],
            compiler_params=params,
        )(position, shift_table, *data)
    return pl.pallas_call(
        functools.partial(back_kernel, bits, merged, largest, corrected),
        out_shape=(
            jax.ShapeDtypeStruct((ROWS, SUB * wide), jnp.bfloat16),
            jax.ShapeDtypeStruct((box_widths.shape[0], ROWS), jnp.float32),
        ),
        in_specs=[smem] * 3 + [vmem] * len(data),
        out_specs=(vmem, vmem),
        scratch_shapes=[levels, pltpu.VMEM((wide // LANES, ROWS * SUB, LANES), jnp.float32)],
        compiler_params=params,
    )(position, shift_table, box_widths, *data)


def shards(filterbank, shift_table, box_widths):
    devices = lax.axis_size("chan")
    all_bits = devices.bit_length() - 1
    me = lax.axis_index("chan")
    bits = min(GROUP_BITS, all_bits)
    rows, correction = front(filterbank, shift_table, bits, filterbank.shape[0] * devices)
    for bit in range(bits, all_bits):
        route = [(source, source ^ 1 << bit) for source in range(devices)]
        correction = correction + lax.ppermute(correction, "chan", route)
    done = 0
    position = jnp.zeros((), jnp.int32)
    while True:
        for bit in range(done, done + bits):
            position = 2 * position + (me >> bit & 1)
        last = done + bits == all_bits
        result = merge(
            rows, correction, shift_table, position[None], bits, 1 << done, box_widths if last else None
        )
        if last:
            return result
        done += bits
        bits = min(GROUP_BITS, all_bits - done)
        rows = exchange(result, bits, 1 << done, done)
        correction = None


def solution(mesh):
    placed = (P(("beam", "chan"), None), P(), P())
    return jax.shard_map(
        shards,
        mesh=mesh,
        in_specs=placed,
        out_specs=(P(("beam", "chan"), None), P("beam", "chan")),
        check_vma=False,
    )
```

```python
import functools

import jax
import jax.numpy as jnp
from jax import lax
from jax.experimental import pallas as pl
from jax.experimental.pallas import tpu as pltpu
from jax.sharding import PartitionSpec as P

ROWS = 16
SUB = 8
LANES = 128
GROUP_BITS = 4

epsilon = 1e-05

VMEM_LIMIT = 48 * 1024 * 1024


def lane_index():
    return lax.broadcasted_iota(jnp.int32, (SUB, LANES), 1)


def next_sublane(tile):
    sub = lax.broadcasted_iota(jnp.int32, tile.shape, tile.ndim - 2)
    return jnp.where(sub == SUB - 1, 0.0, pltpu.roll(tile, SUB - 1, tile.ndim - 2))


def combine(tiles, amount):
    back = (LANES - amount) & (LANES - 1)
    turned = [pltpu.roll(tile, back, tile.ndim - 1) for tile in tiles]
    lane = lax.broadcasted_iota(jnp.int32, tiles[0].shape, tiles[0].ndim - 1)
    keep = lane < LANES - amount
    return [jnp.where(keep, turned[i], turned[i + 1]) for i in range(len(tiles) - 1)]


def advanced(tiles, amount):
    return combine(list(tiles) + [next_sublane(tiles[0])], amount)


def plus(first, second):
    return [a + b for a, b in zip(first, second)]


def digit_bits(digit, bits):
    return [(digit // (1 << i)) % 2 for i in range(bits)]


def partner(bit_values, k):
    flipped = [1 - b if k >> i & 1 else b for i, b in enumerate(bit_values)]
    plain = sum((b * (1 << i) for i, b in enumerate(flipped)), 0)
    turned = sum((b * (1 << len(flipped) - 1 - i) for i, b in enumerate(flipped)), 0)
    return plain, turned


def peer_rounds(bits):
    return sorted(range(1, 1 << bits), reverse=True)


def enter(peers):
    barrier = pltpu.get_barrier_semaphore()
    for peer in peers:
        pl.semaphore_signal(
            barrier, inc=1, device_id={"chan": peer}, device_id_type=pl.DeviceIdType.MESH
        )
    return barrier


def remote(src, dst, send_sem, recv_sem, k, peer):
    return pltpu.make_async_remote_copy(
        src_ref=src,
        dst_ref=dst,
        send_sem=send_sem.at[k],
        recv_sem=recv_sem.at[k],
        device_id={"chan": peer},
        device_id_type=pl.DeviceIdType.MESH,
    )


def front_kernel(
    bits, total_channels, fb_far, table_far, rows, mean_row,
    fb, table, in_sem, table_sem, norm, base, level2, level4, level8, send, pieces, landed, gathered,
    scat_send, scat_recv, gath_send, gath_recv, row_send, row_recv, own_sem,
):
    group = 1 << bits
    held = ROWS // group
    channels, length = fb.shape
    wide = length // SUB
    count = wide // LANES
    step = 16
    arrivals = []
    for n, first in enumerate(range(0, channels, step)):
        block = pl.ds(first, step)
        arrivals.append(pltpu.make_async_copy(fb_far.at[block], fb.at[block], in_sem.at[n]))
    table_in = pltpu.make_async_copy(table_far, table, table_sem)
    for arrival in arrivals:
        arrival.start()
    table_in.start()
    me = lax.axis_index("chan")
    digit = me % group
    mine = digit_bits(digit, bits)
    _, my_turn = partner(mine, 0)
    rounds = peer_rounds(bits)
    peers = {}
    for k in rounds:
        plain, turned = partner(mine, k)
        peers[k] = (me - digit + plain, plain, turned)
    barrier = enter([peers[k][0] for k in rounds])

    for arrival, first in zip(arrivals, range(0, channels, step)):
        arrival.wait()
        values = fb[first : first + step, :].astype(jnp.float32)
        centre = jnp.mean(values, axis=1, keepdims=True)
        moved = values - centre
        spread = jnp.mean(jnp.square(moved), axis=1, keepdims=True)
        scaled = moved * lax.rsqrt(spread + epsilon)
        for s in range(SUB):
            for m in range(count):
                at = s * wide + m * LANES
                norm[m, pl.ds(first * SUB + s, step, stride=SUB), :] = scaled[:, at : at + LANES]

    table_in.wait()
    single = table[0]
    partial = None
    for q in range(channels // 4):
        row = []
        for c in range(4):
            at = (4 * q + c) * SUB
            row.append([norm[m, at : at + SUB, :] for m in range(count)])
        summed = plus(plus(row[0], row[1]), plus(row[2], row[3]))
        partial = summed if partial is None else plus(partial, summed)
        low = plus(row[0], advanced(row[1], single))
        high = plus(row[2], advanced(row[3], single))
        merged = plus(low, advanced(high, single))
        for m in range(count):
            base[q, :, m * LANES : (m + 1) * LANES] = merged[m]
    for e in range(ROWS):
        s, m = 2 * (e // count), e % count
        pieces[e] = partial[m][s : s + 2, :]

    if rounds:
        pl.semaphore_wait(barrier, len(rounds))
    scatter = {}
    for k in rounds:
        chan, plain, turned = peers[k]
        scatter[k] = remote(
            pieces.at[pl.ds(plain * held, held)], landed.at[digit], scat_send, scat_recv, k, chan
        )
        scatter[k].start()

    def tiles_of(load):
        return [load(slice(m * LANES, (m + 1) * LANES)) for m in range(count)]

    subs = channels // 4
    view = base.reshape(subs // 2, 2, 1, SUB, wide)
    trials = 1
    for target in (level2, level4, level8, send):
        trials *= 2
        subs //= 2
        for i in range(trials):
            low = tiles_of(lambda w: view[:, 0, i // 2, :, w])
            high = tiles_of(lambda w: view[:, 1, i // 2, :, w])
            merged = plus(low, advanced(high, table[trials - 1 + i]))
            for m in range(count):
                w = slice(m * LANES, (m + 1) * LANES)
                if subs > 1:
                    target[:, i, :, w] = merged[m]
                else:
                    target[i, :, w] = merged[m][0]
        if subs > 1:
            view = target.reshape(subs // 2, 2, trials, SUB, wide)

    copies = {}
    for k in rounds:
        chan, plain, turned = peers[k]
        copies[k] = remote(
            send.at[pl.ds(turned * held, held)], rows.at[pl.ds(digit * held, held)], row_send, row_recv, k, chan
        )
        copies[k].start()
    own = pltpu.make_async_copy(
        send.at[pl.ds(my_turn * held, held)], rows.at[pl.ds(digit * held, held)], own_sem
    )
    own.start()

    total = pieces[pl.ds(digit * held, held)]
    for k in rounds:
        scatter[k].wait_recv()
        total = total + landed[peers[k][1]]
    gathered[pl.ds(digit * held, held)] = total * (1.0 / total_channels)
    gather = {}
    for k in rounds:
        here = gathered.at[pl.ds(digit * held, held)]
        gather[k] = remote(here, here, gath_send, gath_recv, k, peers[k][0])
        gather[k].start()
    for k in rounds:
        gather[k].wait_recv()
    mean = []
    for m in range(count):
        mean.append(jnp.concatenate([gathered[a * count + m] for a in range(SUB // 2)], axis=0))

    for j in range(held):
        trial = my_turn * held + j
        line = plus(mean, advanced(mean, single))
        line = plus(line, advanced(line, single))
        for level in range(1, 5):
            now = trial // (1 << 4 - level)
            line = plus(line, advanced(line, table[(1 << level) - 1 + now]))
        for m in range(count):
            mean_row[j, :, m * LANES : (m + 1) * LANES] = line[m]

    own.wait()
    for k in rounds:
        copies[k].wait_recv()
    for k in rounds:
        scatter[k].wait_send()
        gather[k].wait_send()
        copies[k].wait_send()


def front(filterbank, shift_table, bits, total_channels):
    channels, length = filterbank.shape
    wide = length // SUB
    group = 1 << bits
    held = ROWS // group
    f32 = jnp.float32
    return pl.pallas_call(
        functools.partial(front_kernel, bits, total_channels),
        out_shape=(
            jax.ShapeDtypeStruct((ROWS, SUB, wide), f32),
            jax.ShapeDtypeStruct((held, SUB, wide), f32),
        ),
        in_specs=[pl.BlockSpec(memory_space=pltpu.HBM)] * 2,
        out_specs=(pl.BlockSpec(memory_space=pl.ANY), pl.BlockSpec(memory_space=pltpu.VMEM)),
        scratch_shapes=[
            pltpu.VMEM(filterbank.shape, filterbank.dtype),
            pltpu.SMEM(shift_table.shape, shift_table.dtype),
            pltpu.SemaphoreType.DMA((channels // 16,)),
            pltpu.SemaphoreType.DMA,
            pltpu.VMEM((wide // LANES, channels * SUB, LANES), f32),
            pltpu.VMEM((16, SUB, wide), f32),
            pltpu.VMEM((8, 2, SUB, wide), f32),
            pltpu.VMEM((4, 4, SUB, wide), f32),
            pltpu.VMEM((2, 8, SUB, wide), f32),
            pltpu.VMEM((ROWS, SUB, wide), f32),
            pltpu.VMEM((ROWS, 2, LANES), f32),
            pltpu.VMEM((group, held, 2, LANES), f32),
            pltpu.VMEM((ROWS, 2, LANES), f32),
        ]
        + [pltpu.SemaphoreType.DMA((group,))] * 6
        + [pltpu.SemaphoreType.DMA],
        compiler_params=pltpu.CompilerParams(
            collective_id=0, has_side_effects=True, vmem_limit_bytes=VMEM_LIMIT
        ),
    )(filterbank, shift_table)


def exchange_kernel(bits, stride, block, rows, row_send, row_recv, own_sem):
    group = 1 << bits
    held = ROWS // group
    me = lax.axis_index("chan")
    digit = (me // stride) % group
    mine = digit_bits(digit, bits)
    _, my_turn = partner(mine, 0)
    rounds = peer_rounds(bits)
    peers = {}
    for k in rounds:
        plain, turned = partner(mine, k)
        peers[k] = (me + (plain - digit) * stride, turned)
    barrier = enter([peers[k][0] for k in rounds])
    pl.semaphore_wait(barrier, len(rounds))
    there = rows.at[pl.ds(digit * held, held)]
    copies = {}
    for k in rounds:
        chan, turned = peers[k]
        copies[k] = remote(block.at[pl.ds(turned * held, held)], there, row_send, row_recv, k, chan)
        copies[k].start()
    own = pltpu.make_async_copy(block.at[pl.ds(my_turn * held, held)], there, own_sem)
    own.start()
    own.wait()
    for k in rounds:
        copies[k].wait()


def exchange(block, bits, stride, number):
    group = 1 << bits
    return pl.pallas_call(
        functools.partial(exchange_kernel, bits, stride),
        out_shape=jax.ShapeDtypeStruct(block.shape, block.dtype),
        in_specs=[pl.BlockSpec(memory_space=pltpu.VMEM)],
        out_specs=pl.BlockSpec(memory_space=pl.ANY),
        scratch_shapes=[pltpu.SemaphoreType.DMA((group,))] * 2 + [pltpu.SemaphoreType.DMA],
        compiler_params=pltpu.CompilerParams(
            collective_id=number, has_side_effects=True, vmem_limit_bytes=VMEM_LIMIT
        ),
    )(block)


def merge_rows(bits, merged, largest, block, correction, table_in, table, place, levels, keep):
    group = 1 << bits
    held = ROWS // group
    wide = block.shape[-1]
    count = wide // LANES
    sub = lax.broadcasted_iota(jnp.int32, (SUB, LANES), 0)

    def put(level, row, tiles, is_upper):
        if level == bits:
            keep(row, tiles)
            return
        for m in range(count):
            levels[level][row, :, m * LANES : (m + 1) * LANES] = tiles[m]
            if is_upper:
                levels[level][row, :, wide + m * LANES : wide + (m + 1) * LANES] = next_sublane(tiles[m])

    for row in range(ROWS):
        tiles = []
        for m in range(count):
            w = slice(m * LANES, (m + 1) * LANES)
            tile = block[row, :, w]
            tiles.append(tile if correction is None else tile - correction[row % held, :, w])
        put(0, row, tiles, row // held % 2 == 1)
    table_in.wait()
    trials = held
    for level in range(bits):
        now = 2 * trials
        whole = merged * ROWS << level + 1
        source = levels[level]
        pairs = [(q, i) for i in range(now) for q in range(ROWS // now)]
        for first in range(0, ROWS, 8):
            made = []
            for q, i in pairs[first : first + 8]:
                shift = table[whole - 1 + place * now + i]
                within = shift & (wide - 1)
                at = within // LANES
                low = 2 * q * trials + i // 2
                high = low + trials
                tiles = [
                    source[high, :, pl.ds(pl.multiple_of((at + m) * LANES, LANES), LANES)]
                    for m in range(count + 1)
                ]
                moved = combine(tiles, within & (LANES - 1))
                if largest >= wide:
                    up = jnp.minimum(shift // wide, SUB)
                    moved = [
                        jnp.where(sub < SUB - up, pltpu.roll(tile, (SUB - up) & (SUB - 1), 0), 0.0)
                        for tile in moved
                    ]
                lower = [source[low, :, m * LANES : (m + 1) * LANES] for m in range(count)]
                made.append((q * now + i, plus(lower, moved), q % 2 == 1))
            for row, tiles, is_upper in made:
                put(level + 1, row, tiles, is_upper)
        trials = now


def stage_position(merged, bits):
    me = lax.axis_index("chan")
    known = merged.bit_length() - 1 + bits
    return partner(digit_bits(me, known), 0)[1]


def middle_kernel(bits, merged, largest, corrected, table_far, block, *rest):
    correction = rest[0] if corrected else None
    out, table, table_sem = rest[corrected : corrected + 3]
    levels = rest[corrected + 3 :]
    table_in = pltpu.make_async_copy(table_far, table, table_sem)
    table_in.start()

    def keep(row, tiles):
        for m in range(len(tiles)):
            out[row, :, m * LANES : (m + 1) * LANES] = tiles[m]

    place = stage_position(merged, bits)
    merge_rows(bits, merged, largest, block, correction, table_in, table, place, levels, keep)


def back_kernel(bits, merged, largest, corrected, table_far, widths_far, block, *rest):
    correction = rest[0] if corrected else None
    dedispersed, peaks, flat, widths, widths_sem, table, table_sem = rest[corrected : corrected + 7]
    levels = rest[corrected + 7 :]
    wide = block.shape[-1]
    length = wide * SUB
    table_in = pltpu.make_async_copy(table_far, table, table_sem)
    widths_in = pltpu.make_async_copy(widths_far, widths, widths_sem)
    table_in.start()
    widths_in.start()

    def keep(row, tiles):
        for m in range(len(tiles)):
            flat[m, row * SUB : (row + 1) * SUB, :] = tiles[m]

    place = stage_position(merged, bits)
    merge_rows(bits, merged, largest, block, correction, table_in, table, place, levels, keep)
    series = [
        jnp.concatenate([flat[m, pl.ds(s, ROWS, stride=SUB), :] for m in range(wide // LANES)], axis=1)
        for s in range(SUB)
    ]
    summed = series[0]
    for part in series[1:]:
        summed = summed + part
    centre = jnp.sum(summed, axis=1, keepdims=True) * (1.0 / length)
    series = [part - centre for part in series]
    squared = jnp.square(series[0])
    for part in series[1:]:
        squared = squared + jnp.square(part)
    spread = jnp.sum(squared, axis=1, keepdims=True) * (1.0 / length)
    factor = lax.rsqrt(spread + epsilon)
    series = [part * factor for part in series]
    for s in range(SUB):
        dedispersed[:, s * wide : (s + 1) * wide] = series[s].astype(jnp.bfloat16)

    piece = 2 * LANES
    stacked = jnp.concatenate(
        [part[:, a : a + piece] for part in series for a in range(0, wide, piece)], axis=0
    )
    triangle = jnp.where(
        lax.broadcasted_iota(jnp.int32, (piece, piece + LANES), 0)
        <= lax.broadcasted_iota(jnp.int32, (piece, piece + LANES), 1),
        1.0,
        0.0,
    ).astype(jnp.bfloat16)
    rest_value = stacked
    inner = None
    for _ in range(3):
        top = rest_value.astype(jnp.bfloat16)
        rest_value = rest_value - top.astype(jnp.float32)
        product = jnp.dot(top, triangle, preferred_element_type=jnp.float32)
        inner = product if inner is None else inner + product
    offset = jnp.zeros((ROWS, LANES), jnp.float32)
    prefix = []
    for p in range(length // piece):
        one = inner[p * ROWS : (p + 1) * ROWS, :]
        prefix += [one[:, :LANES] + offset, one[:, LANES:piece] + offset]
        offset = offset + one[:, piece:]

    lane = lax.broadcasted_iota(jnp.int32, (ROWS, LANES), 1)
    diagonal = lane == lax.broadcasted_iota(jnp.int32, (ROWS, LANES), 0)
    zero = jnp.zeros((ROWS, LANES), jnp.float32)
    count = peaks.shape[0]
    widths_in.wait()
    for i in range(count):
        width = widths[i]
        whole, amount = divmod(1 << i, LANES)
        amount = width - whole * LANES
        keep = lane >= amount
        best = None
        before = zero
        for c in range(len(prefix)):
            source = c - whole
            now = pltpu.roll(prefix[source], amount, 1) if source >= 0 else zero
            box = prefix[c] - jnp.where(keep, now, before)
            before = now
            best = box if best is None else jnp.maximum(best, box)
        root = lax.rsqrt(jnp.full((ROWS, 1), width, jnp.int32).astype(jnp.float32))
        column = jnp.max(best, axis=1, keepdims=True) * root
        line = jnp.sum(jnp.where(diagonal, column, 0.0), axis=0, keepdims=True)
        peaks[i : i + 1, :] = line[:, :ROWS]


def merge(block, correction, shift_table, bits, merged, box_widths):
    wide = block.shape[-1]
    largest = 2 * ((merged * ROWS << bits) - 1) + 1
    corrected = correction is not None
    far = pl.BlockSpec(memory_space=pltpu.HBM)
    vmem = pl.BlockSpec(memory_space=pltpu.VMEM)
    levels = [pltpu.VMEM((ROWS, SUB, 2 * wide), jnp.float32)] * bits
    table = [pltpu.SMEM(shift_table.shape, shift_table.dtype), pltpu.SemaphoreType.DMA]
    params = pltpu.CompilerParams(vmem_limit_bytes=VMEM_LIMIT)
    data = (block, correction) if corrected else (block,)
    if box_widths is None:
        return pl.pallas_call(
            functools.partial(middle_kernel, bits, merged, largest, corrected),
            out_shape=jax.ShapeDtypeStruct(block.shape, jnp.float32),
            in_specs=[far] + [vmem] * len(data),
            out_specs=vmem,
            scratch_shapes=table + levels,
            compiler_params=params,
        )(shift_table, *data)
    widths = [pltpu.SMEM(box_widths.shape, box_widths.dtype), pltpu.SemaphoreType.DMA]
    return pl.pallas_call(
        functools.partial(back_kernel, bits, merged, largest, corrected),
        out_shape=(
            jax.ShapeDtypeStruct((ROWS, SUB * wide), jnp.bfloat16),
            jax.ShapeDtypeStruct((box_widths.shape[0], ROWS), jnp.float32),
        ),
        in_specs=[far] * 2 + [vmem] * len(data),
        out_specs=(vmem, vmem),
        scratch_shapes=[pltpu.VMEM((wide // LANES, ROWS * SUB, LANES), jnp.float32)] + widths + table + levels,
        compiler_params=params,
    )(shift_table, box_widths, *data)


def shards(filterbank, shift_table, box_widths):
    devices = lax.axis_size("chan")
    all_bits = devices.bit_length() - 1
    bits = min(GROUP_BITS, all_bits)
    rows, correction = front(filterbank, shift_table, bits, filterbank.shape[0] * devices)
    for bit in range(bits, all_bits):
        route = [(source, source ^ 1 << bit) for source in range(devices)]
        correction = correction + lax.ppermute(correction, "chan", route)
    done = 0
    while True:
        last = done + bits == all_bits
        result = merge(rows, correction, shift_table, bits, 1 << done, box_widths if last else None)
        if last:
            return result
        done += bits
        bits = min(GROUP_BITS, all_bits - done)
        rows = exchange(result, bits, 1 << done, done)
        correction = None


def solution(mesh):
    placed = (P(("beam", "chan"), None), P(), P())
    return jax.shard_map(
        shards,
        mesh=mesh,
        in_specs=placed,
        out_specs=(P(("beam", "chan"), None), P("beam", "chan")),
        check_vma=False,
    )
```

```python
import functools

import jax
import jax.numpy as jnp
from jax import lax
from jax.experimental import pallas as pl
from jax.experimental.pallas import tpu as pltpu
from jax.sharding import PartitionSpec as P

ROWS = 16
SUB = 8
LANES = 128
GROUP_BITS = 4

epsilon = 1e-05

VMEM_LIMIT = 48 * 1024 * 1024


def lane_index():
    return lax.broadcasted_iota(jnp.int32, (SUB, LANES), 1)


def next_sublane(tile):
    sub = lax.broadcasted_iota(jnp.int32, tile.shape, tile.ndim - 2)
    return jnp.where(sub == SUB - 1, 0.0, pltpu.roll(tile, SUB - 1, tile.ndim - 2))


def combine(tiles, amount):
    back = (LANES - amount) & (LANES - 1)
    turned = [pltpu.roll(tile, back, tile.ndim - 1) for tile in tiles]
    lane = lax.broadcasted_iota(jnp.int32, tiles[0].shape, tiles[0].ndim - 1)
    keep = lane < LANES - amount
    return [jnp.where(keep, turned[i], turned[i + 1]) for i in range(len(tiles) - 1)]


def advanced(tiles, amount):
    return combine(list(tiles) + [next_sublane(tiles[0])], amount)


def plus(first, second):
    return [a + b for a, b in zip(first, second)]


def digit_bits(digit, bits):
    return [(digit // (1 << i)) % 2 for i in range(bits)]


def partner(bit_values, k):
    flipped = [1 - b if k >> i & 1 else b for i, b in enumerate(bit_values)]
    plain = sum((b * (1 << i) for i, b in enumerate(flipped)), 0)
    turned = sum((b * (1 << len(flipped) - 1 - i) for i, b in enumerate(flipped)), 0)
    return plain, turned


def peer_rounds(bits):
    return sorted(range(1, 1 << bits), reverse=True)


def enter(peers):
    barrier = pltpu.get_barrier_semaphore()
    for peer in peers:
        pl.semaphore_signal(
            barrier, inc=1, device_id={"chan": peer}, device_id_type=pl.DeviceIdType.MESH
        )
    return barrier


def remote(src, dst, send_sem, recv_sem, k, peer):
    return pltpu.make_async_remote_copy(
        src_ref=src,
        dst_ref=dst,
        send_sem=send_sem.at[k],
        recv_sem=recv_sem.at[k],
        device_id={"chan": peer},
        device_id_type=pl.DeviceIdType.MESH,
    )


def front_kernel(
    bits, total_channels, whole, fb_far, table_far, widths_far, *rest,
):
    if whole:
        dedispersed, peaks, rows, mean_row, flat, *rest = rest
    else:
        rows, mean_row, *rest = rest
    front_steps(
        bits, total_channels, fb_far, table_far, widths_far, rows, mean_row,
        (dedispersed, peaks, flat) if whole else None, *rest
    )


def front_steps(
    bits, total_channels, fb_far, table_far, widths_far, rows, mean_row, ending,
    widths, widths_sem, fb, table, in_sem, table_sem, norm, base, level2, level4, level8, send, pieces, landed, gathered,
    scat_send, scat_recv, gath_send, gath_recv, row_send, row_recv, own_sem, *levels,
):
    group = 1 << bits
    held = ROWS // group
    channels, length = fb.shape
    wide = length // SUB
    count = wide // LANES
    step = 16
    arrivals = []
    for n, first in enumerate(range(0, channels, step)):
        block = pl.ds(first, step)
        arrivals.append(pltpu.make_async_copy(fb_far.at[block], fb.at[block], in_sem.at[n]))
    table_in = pltpu.make_async_copy(table_far, table, table_sem)
    for arrival in arrivals:
        arrival.start()
    table_in.start()
    if ending:
        widths_in = pltpu.make_async_copy(widths_far, widths, widths_sem)
        widths_in.start()
    me = lax.axis_index("chan")
    digit = me % group
    mine = digit_bits(digit, bits)
    _, my_turn = partner(mine, 0)
    rounds = peer_rounds(bits)
    peers = {}
    for k in rounds:
        plain, turned = partner(mine, k)
        peers[k] = (me - digit + plain, plain, turned)
    barrier = enter([peers[k][0] for k in rounds])

    for arrival, first in zip(arrivals, range(0, channels, step)):
        arrival.wait()
        values = fb[first : first + step, :].astype(jnp.float32)
        centre = jnp.mean(values, axis=1, keepdims=True)
        moved = values - centre
        spread = jnp.mean(jnp.square(moved), axis=1, keepdims=True)
        scaled = moved * lax.rsqrt(spread + epsilon)
        for s in range(SUB):
            for m in range(count):
                at = s * wide + m * LANES
                norm[m, pl.ds(first * SUB + s, step, stride=SUB), :] = scaled[:, at : at + LANES]

    partial = None
    for c in range(channels):
        row = [norm[m, c * SUB : (c + 1) * SUB, :] for m in range(count)]
        partial = row if partial is None else plus(partial, row)
    for e in range(ROWS):
        s, m = 2 * (e // count), e % count
        pieces[e] = partial[m][s : s + 2, :]
    if rounds:
        pl.semaphore_wait(barrier, len(rounds))
    scatter = {}
    for k in rounds:
        chan, plain, turned = peers[k]
        scatter[k] = remote(
            pieces.at[pl.ds(plain * held, held)], landed.at[digit], scat_send, scat_recv, k, chan
        )
        scatter[k].start()

    table_in.wait()
    single = table[0]
    for q in range(channels // 4):
        row = []
        for c in range(4):
            at = (4 * q + c) * SUB
            row.append([norm[m, at : at + SUB, :] for m in range(count)])
        low = plus(row[0], advanced(row[1], single))
        high = plus(row[2], advanced(row[3], single))
        merged = plus(low, advanced(high, single))
        for m in range(count):
            base[q, :, m * LANES : (m + 1) * LANES] = merged[m]

    def tiles_of(load):
        return [load(slice(m * LANES, (m + 1) * LANES)) for m in range(count)]

    subs = channels // 4
    view = base.reshape(subs // 2, 2, 1, SUB, wide)
    trials = 1
    for target in (level2, level4, level8, send):
        trials *= 2
        subs //= 2
        for i in range(trials):
            low = tiles_of(lambda w: view[:, 0, i // 2, :, w])
            high = tiles_of(lambda w: view[:, 1, i // 2, :, w])
            merged = plus(low, advanced(high, table[trials - 1 + i]))
            for m in range(count):
                w = slice(m * LANES, (m + 1) * LANES)
                if subs > 1:
                    target[:, i, :, w] = merged[m]
                else:
                    target[i, :, w] = merged[m][0]
        if subs > 1:
            view = target.reshape(subs // 2, 2, trials, SUB, wide)

    total = pieces[pl.ds(digit * held, held)]
    for k in rounds:
        scatter[k].wait_recv()
        total = total + landed[peers[k][1]]
    gathered[pl.ds(digit * held, held)] = total * (1.0 / total_channels)
    gather = {}
    for k in rounds:
        here = gathered.at[pl.ds(digit * held, held)]
        gather[k] = remote(here, here, gath_send, gath_recv, k, peers[k][0])
        gather[k].start()
    copies = {}
    for k in rounds:
        chan, plain, turned = peers[k]
        copies[k] = remote(
            send.at[pl.ds(turned * held, held)], rows.at[pl.ds(digit * held, held)], row_send, row_recv, k, chan
        )
        copies[k].start()
    if ending:
        rows[pl.ds(digit * held, held)] = send[pl.ds(my_turn * held, held)]
    else:
        own = pltpu.make_async_copy(
            send.at[pl.ds(my_turn * held, held)], rows.at[pl.ds(digit * held, held)], own_sem
        )
        own.start()

    for k in rounds:
        gather[k].wait_recv()
    mean = []
    for m in range(count):
        mean.append(jnp.concatenate([gathered[a * count + m] for a in range(SUB // 2)], axis=0))

    for j in range(held):
        trial = my_turn * held + j
        line = plus(mean, advanced(mean, single))
        line = plus(line, advanced(line, single))
        for level in range(1, 5):
            now = trial // (1 << 4 - level)
            line = plus(line, advanced(line, table[(1 << level) - 1 + now]))
        for m in range(count):
            mean_row[j, :, m * LANES : (m + 1) * LANES] = line[m]

    if ending:
        dedispersed, peaks, flat = ending
        half = mine[bits - 1]

        def near():
            for k in rounds:
                if k < group // 2:
                    copies[k].wait_recv()

        def far():
            for k in rounds:
                if k >= group // 2:
                    copies[k].wait_recv()

        def keep(row, tiles):
            for m in range(count):
                flat[m, row * SUB : (row + 1) * SUB, :] = tiles[m]

        halves = [(half * (ROWS // 2), near), ((1 - half) * (ROWS // 2), far)]
        largest = 2 * (ROWS * group - 1) + 1
        merge_rows(bits, 1, largest, rows, mean_row, table, my_turn, levels, keep, halves)
        finish(length, flat, widths_in, widths, dedispersed, peaks)
    else:
        own.wait()
        for k in rounds:
            copies[k].wait_recv()
    for k in rounds:
        scatter[k].wait_send()
        gather[k].wait_send()
        copies[k].wait_send()


def front(filterbank, shift_table, box_widths, bits, total_channels, whole):
    channels, length = filterbank.shape
    wide = length // SUB
    group = 1 << bits
    held = ROWS // group
    f32 = jnp.float32
    vmem = pl.BlockSpec(memory_space=pltpu.VMEM)
    if whole:
        results = (
            jax.ShapeDtypeStruct((ROWS, length), jnp.bfloat16),
            jax.ShapeDtypeStruct((box_widths.shape[0], ROWS), f32),
        )
        places = (vmem, vmem)
        kept = [
            pltpu.VMEM((ROWS, SUB, wide), f32),
            pltpu.VMEM((held, SUB, wide), f32),
            pltpu.VMEM((wide // LANES, ROWS * SUB, LANES), f32),
        ]
        levels = [pltpu.VMEM((ROWS, SUB, 2 * wide), f32)] * bits
    else:
        results = (
            jax.ShapeDtypeStruct((ROWS, SUB, wide), f32),
            jax.ShapeDtypeStruct((held, SUB, wide), f32),
        )
        places = (pl.BlockSpec(memory_space=pl.ANY), vmem)
        kept, levels = [], []
    return pl.pallas_call(
        functools.partial(front_kernel, bits, total_channels, whole),
        out_shape=results,
        in_specs=[pl.BlockSpec(memory_space=pltpu.HBM)] * 3,
        out_specs=places,
        scratch_shapes=kept
        + [
            pltpu.SMEM(box_widths.shape, box_widths.dtype),
            pltpu.SemaphoreType.DMA,
            pltpu.VMEM(filterbank.shape, filterbank.dtype),
            pltpu.SMEM(shift_table.shape, shift_table.dtype),
            pltpu.SemaphoreType.DMA((channels // 16,)),
            pltpu.SemaphoreType.DMA,
            pltpu.VMEM((wide // LANES, channels * SUB, LANES), f32),
            pltpu.VMEM((16, SUB, wide), f32),
            pltpu.VMEM((8, 2, SUB, wide), f32),
            pltpu.VMEM((4, 4, SUB, wide), f32),
            pltpu.VMEM((2, 8, SUB, wide), f32),
            pltpu.VMEM((ROWS, SUB, wide), f32),
            pltpu.VMEM((ROWS, 2, LANES), f32),
            pltpu.VMEM((group, held, 2, LANES), f32),
            pltpu.VMEM((ROWS, 2, LANES), f32),
        ]
        + [pltpu.SemaphoreType.DMA((group,))] * 6
        + [pltpu.SemaphoreType.DMA]
        + levels,
        compiler_params=pltpu.CompilerParams(collective_id=0, has_side_effects=True),
    )(filterbank, shift_table, box_widths)


def exchange_kernel(bits, stride, block, rows, row_send, row_recv, own_sem):
    group = 1 << bits
    held = ROWS // group
    me = lax.axis_index("chan")
    digit = (me // stride) % group
    mine = digit_bits(digit, bits)
    _, my_turn = partner(mine, 0)
    rounds = peer_rounds(bits)
    peers = {}
    for k in rounds:
        plain, turned = partner(mine, k)
        peers[k] = (me + (plain - digit) * stride, turned)
    barrier = enter([peers[k][0] for k in rounds])
    pl.semaphore_wait(barrier, len(rounds))
    there = rows.at[pl.ds(digit * held, held)]
    copies = {}
    for k in rounds:
        chan, turned = peers[k]
        copies[k] = remote(block.at[pl.ds(turned * held, held)], there, row_send, row_recv, k, chan)
        copies[k].start()
    own = pltpu.make_async_copy(block.at[pl.ds(my_turn * held, held)], there, own_sem)
    own.start()
    own.wait()
    for k in rounds:
        copies[k].wait()


def exchange(block, bits, stride, number):
    group = 1 << bits
    return pl.pallas_call(
        functools.partial(exchange_kernel, bits, stride),
        out_shape=jax.ShapeDtypeStruct(block.shape, block.dtype),
        in_specs=[pl.BlockSpec(memory_space=pltpu.VMEM)],
        out_specs=pl.BlockSpec(memory_space=pl.ANY),
        scratch_shapes=[pltpu.SemaphoreType.DMA((group,))] * 2 + [pltpu.SemaphoreType.DMA],
        compiler_params=pltpu.CompilerParams(
            collective_id=number, has_side_effects=True, vmem_limit_bytes=VMEM_LIMIT
        ),
    )(block)


def merge_rows(bits, merged, largest, block, correction, table, place, levels, keep, halves):
    group = 1 << bits
    held = ROWS // group
    wide = block.shape[-1]
    count = wide // LANES
    sub = lax.broadcasted_iota(jnp.int32, (SUB, LANES), 0)

    def put(level, row, tiles, is_upper):
        if level == bits:
            keep(row, tiles)
            return
        for m in range(count):
            levels[level][row, :, m * LANES : (m + 1) * LANES] = tiles[m]
            if is_upper and m * LANES < 2 * (merged * ROWS << level + 1):
                levels[level][row, :, wide + m * LANES : wide + (m + 1) * LANES] = next_sublane(tiles[m])

    def load(base):
        for c in range(ROWS // 2):
            tiles = []
            for m in range(count):
                w = slice(m * LANES, (m + 1) * LANES)
                tile = block[base + c, :, w]
                tiles.append(tile if correction is None else tile - correction[c % held, :, w])
            put(0, base + c, tiles, c // held % 2 == 1)

    def run(level, base, size):
        trials = held << level
        now = 2 * trials
        whole = merged * ROWS << level + 1
        source = levels[level]
        start = 2 * now * place
        at = start % wide // LANES
        pairs = [(q, i) for i in range(now) for q in range(size // now)]
        for first in range(0, size, 8):
            made = []
            for q, i in pairs[first : first + 8]:
                shift = table[whole - 1 + place * now + i]
                low = base + 2 * q * trials + i // 2
                high = low + trials
                tiles = [
                    source[high, :, pl.ds(pl.multiple_of((at + m) * LANES, LANES), LANES)]
                    for m in range(count + 1)
                ]
                moved = combine(tiles, shift & (LANES - 1))
                if largest >= wide:
                    up = jnp.minimum(start // wide, SUB)
                    moved = [
                        jnp.where(sub < SUB - up, pltpu.roll(tile, (SUB - up) & (SUB - 1), 0), 0.0)
                        for tile in moved
                    ]
                lower = [source[low, :, m * LANES : (m + 1) * LANES] for m in range(count)]
                made.append((base + q * now + i, plus(lower, moved), q % 2 == 1 or now == size))
            for row, tiles, is_upper in made:
                put(level + 1, row, tiles, is_upper)

    for base, ready in halves:
        ready()
        load(base)
        for level in range(bits - 1):
            run(level, base, ROWS // 2)
    run(bits - 1, 0, ROWS)


def stage_position(merged, bits):
    me = lax.axis_index("chan")
    known = merged.bit_length() - 1 + bits
    return partner(digit_bits(me, known), 0)[1]


def middle_kernel(bits, merged, largest, corrected, table_far, block, *rest):
    correction = rest[0] if corrected else None
    out, table, table_sem = rest[corrected : corrected + 3]
    levels = rest[corrected + 3 :]
    table_in = pltpu.make_async_copy(table_far, table, table_sem)
    table_in.start()

    def keep(row, tiles):
        for m in range(len(tiles)):
            out[row, :, m * LANES : (m + 1) * LANES] = tiles[m]

    place = stage_position(merged, bits)
    halves = [(0, table_in.wait), (ROWS // 2, lambda: None)]
    merge_rows(bits, merged, largest, block, correction, table, place, levels, keep, halves)


def back_kernel(bits, merged, largest, corrected, table_far, widths_far, block, *rest):
    correction = rest[0] if corrected else None
    dedispersed, peaks, flat, widths, widths_sem, table, table_sem = rest[corrected : corrected + 7]
    levels = rest[corrected + 7 :]
    wide = block.shape[-1]
    length = wide * SUB
    table_in = pltpu.make_async_copy(table_far, table, table_sem)
    widths_in = pltpu.make_async_copy(widths_far, widths, widths_sem)
    table_in.start()
    widths_in.start()

    def keep(row, tiles):
        for m in range(len(tiles)):
            flat[m, row * SUB : (row + 1) * SUB, :] = tiles[m]

    place = stage_position(merged, bits)
    halves = [(0, table_in.wait), (ROWS // 2, lambda: None)]
    merge_rows(bits, merged, largest, block, correction, table, place, levels, keep, halves)
    finish(length, flat, widths_in, widths, dedispersed, peaks)


def finish(length, flat, widths_in, widths, dedispersed, peaks):
    wide = length // SUB
    series = [
        jnp.concatenate([flat[m, pl.ds(s, ROWS, stride=SUB), :] for m in range(wide // LANES)], axis=1)
        for s in range(SUB)
    ]
    summed = series[0]
    for part in series[1:]:
        summed = summed + part
    centre = jnp.sum(summed, axis=1, keepdims=True) * (1.0 / length)
    series = [part - centre for part in series]
    squared = jnp.square(series[0])
    for part in series[1:]:
        squared = squared + jnp.square(part)
    spread = jnp.sum(squared, axis=1, keepdims=True) * (1.0 / length)
    factor = lax.rsqrt(spread + epsilon)
    series = [part * factor for part in series]
    for s in range(SUB):
        dedispersed[:, s * wide : (s + 1) * wide] = series[s].astype(jnp.bfloat16)

    piece = 2 * LANES
    stacked = jnp.concatenate(
        [part[:, a : a + piece] for part in series for a in range(0, wide, piece)], axis=0
    )
    triangle = jnp.where(
        lax.broadcasted_iota(jnp.int32, (piece, piece + LANES), 0)
        <= lax.broadcasted_iota(jnp.int32, (piece, piece + LANES), 1),
        1.0,
        0.0,
    ).astype(jnp.bfloat16)
    rest_value = stacked
    inner = None
    for _ in range(3):
        top = rest_value.astype(jnp.bfloat16)
        rest_value = rest_value - top.astype(jnp.float32)
        product = jnp.dot(top, triangle, preferred_element_type=jnp.float32)
        inner = product if inner is None else inner + product
    offset = jnp.zeros((ROWS, LANES), jnp.float32)
    prefix = []
    for p in range(length // piece):
        one = inner[p * ROWS : (p + 1) * ROWS, :]
        prefix += [one[:, :LANES] + offset, one[:, LANES:piece] + offset]
        offset = offset + one[:, piece:]

    lane = lax.broadcasted_iota(jnp.int32, (ROWS, LANES), 1)
    diagonal = lane == lax.broadcasted_iota(jnp.int32, (ROWS, LANES), 0)
    zero = jnp.zeros((ROWS, LANES), jnp.float32)
    count = peaks.shape[0]
    widths_in.wait()
    for i in range(count):
        width = widths[i]
        whole, amount = divmod(1 << i, LANES)
        amount = width - whole * LANES
        keep = lane >= amount
        best = None
        before = zero
        for c in range(len(prefix)):
            source = c - whole
            now = pltpu.roll(prefix[source], amount, 1) if source >= 0 else zero
            box = prefix[c] - jnp.where(keep, now, before)
            before = now
            best = box if best is None else jnp.maximum(best, box)
        root = lax.rsqrt(jnp.full((ROWS, 1), width, jnp.int32).astype(jnp.float32))
        column = jnp.max(best, axis=1, keepdims=True) * root
        line = jnp.sum(jnp.where(diagonal, column, 0.0), axis=0, keepdims=True)
        peaks[i : i + 1, :] = line[:, :ROWS]


def merge(block, correction, shift_table, bits, merged, box_widths):
    wide = block.shape[-1]
    largest = 2 * ((merged * ROWS << bits) - 1) + 1
    corrected = correction is not None
    far = pl.BlockSpec(memory_space=pltpu.HBM)
    vmem = pl.BlockSpec(memory_space=pltpu.VMEM)
    levels = [pltpu.VMEM((ROWS, SUB, 2 * wide), jnp.float32)] * bits
    table = [pltpu.SMEM(shift_table.shape, shift_table.dtype), pltpu.SemaphoreType.DMA]
    params = pltpu.CompilerParams(vmem_limit_bytes=VMEM_LIMIT)
    data = (block, correction) if corrected else (block,)
    if box_widths is None:
        return pl.pallas_call(
            functools.partial(middle_kernel, bits, merged, largest, corrected),
            out_shape=jax.ShapeDtypeStruct(block.shape, jnp.float32),
            in_specs=[far] + [vmem] * len(data),
            out_specs=vmem,
            scratch_shapes=table + levels,
            compiler_params=params,
        )(shift_table, *data)
    widths = [pltpu.SMEM(box_widths.shape, box_widths.dtype), pltpu.SemaphoreType.DMA]
    return pl.pallas_call(
        functools.partial(back_kernel, bits, merged, largest, corrected),
        out_shape=(
            jax.ShapeDtypeStruct((ROWS, SUB * wide), jnp.bfloat16),
            jax.ShapeDtypeStruct((box_widths.shape[0], ROWS), jnp.float32),
        ),
        in_specs=[far] * 2 + [vmem] * len(data),
        out_specs=(vmem, vmem),
        scratch_shapes=[pltpu.VMEM((wide // LANES, ROWS * SUB, LANES), jnp.float32)] + widths + table + levels,
        compiler_params=params,
    )(shift_table, box_widths, *data)


def shards(filterbank, shift_table, box_widths):
    devices = lax.axis_size("chan")
    all_bits = devices.bit_length() - 1
    bits = min(GROUP_BITS, all_bits)
    whole = bits == all_bits
    made = front(filterbank, shift_table, box_widths, bits, filterbank.shape[0] * devices, whole)
    if whole:
        return made
    rows, correction = made
    for bit in range(bits, all_bits):
        route = [(source, source ^ 1 << bit) for source in range(devices)]
        correction = correction + lax.ppermute(correction, "chan", route)
    done = 0
    while True:
        last = done + bits == all_bits
        result = merge(rows, correction, shift_table, bits, 1 << done, box_widths if last else None)
        if last:
            return result
        done += bits
        bits = min(GROUP_BITS, all_bits - done)
        rows = exchange(result, bits, 1 << done, done)
        correction = None


def solution(mesh):
    placed = (P(("beam", "chan"), None), P(), P())
    return jax.shard_map(
        shards,
        mesh=mesh,
        in_specs=placed,
        out_specs=(P(("beam", "chan"), None), P("beam", "chan")),
        check_vma=False,
    )
```

```python
import functools

import jax
import jax.numpy as jnp
from jax import lax
from jax.experimental import pallas as pl
from jax.experimental.pallas import tpu as pltpu
from jax.sharding import PartitionSpec as P

ROWS = 16
SUB = 8
LANES = 128
GROUP_BITS = 4

epsilon = 1e-05


def lane_index():
    return lax.broadcasted_iota(jnp.int32, (SUB, LANES), 1)


def next_sublane(tile):
    sub = lax.broadcasted_iota(jnp.int32, tile.shape, tile.ndim - 2)
    return jnp.where(sub == SUB - 1, 0.0, pltpu.roll(tile, SUB - 1, tile.ndim - 2))


def combine(tiles, amount):
    back = (LANES - amount) & (LANES - 1)
    turned = [pltpu.roll(tile, back, tile.ndim - 1) for tile in tiles]
    lane = lax.broadcasted_iota(jnp.int32, tiles[0].shape, tiles[0].ndim - 1)
    keep = lane < LANES - amount
    return [jnp.where(keep, turned[i], turned[i + 1]) for i in range(len(tiles) - 1)]


def advanced(tiles, amount):
    return combine(list(tiles) + [next_sublane(tiles[0])], amount)


def plus(first, second):
    return [a + b for a, b in zip(first, second)]


def digit_bits(digit, bits):
    return [(digit // (1 << i)) % 2 for i in range(bits)]


def partner(bit_values, k):
    flipped = [1 - b if k >> i & 1 else b for i, b in enumerate(bit_values)]
    plain = sum((b * (1 << i) for i, b in enumerate(flipped)), 0)
    turned = sum((b * (1 << len(flipped) - 1 - i) for i, b in enumerate(flipped)), 0)
    return plain, turned


def peer_rounds(bits):
    return sorted(range(1, 1 << bits), reverse=True)


def enter(peers):
    barrier = pltpu.get_barrier_semaphore()
    for peer in peers:
        pl.semaphore_signal(
            barrier, inc=1, device_id={"chan": peer}, device_id_type=pl.DeviceIdType.MESH
        )
    return barrier


def remote(src, dst, send_sem, recv_sem, k, peer):
    return pltpu.make_async_remote_copy(
        src_ref=src,
        dst_ref=dst,
        send_sem=send_sem.at[k],
        recv_sem=recv_sem.at[k],
        device_id={"chan": peer},
        device_id_type=pl.DeviceIdType.MESH,
    )


def front_kernel(
    bits, total_channels, fb_far, table_far, rows, mean_row,
    fb, table, in_sem, table_sem, norm, base, level2, level4, level8, send, pieces, landed, gathered,
    scat_send, scat_recv, gath_send, gath_recv, row_send, row_recv, own_sem,
):
    group = 1 << bits
    held = ROWS // group
    channels, length = fb.shape
    wide = length // SUB
    count = wide // LANES
    step = 16
    arrivals = []
    for n, first in enumerate(range(0, channels, step)):
        block = pl.ds(first, step)
        arrivals.append(pltpu.make_async_copy(fb_far.at[block], fb.at[block], in_sem.at[n]))
    table_in = pltpu.make_async_copy(table_far, table, table_sem)
    for arrival in arrivals:
        arrival.start()
    table_in.start()
    me = lax.axis_index("chan")
    digit = me % group
    mine = digit_bits(digit, bits)
    _, my_turn = partner(mine, 0)
    rounds = peer_rounds(bits)
    peers = {}
    for k in rounds:
        plain, turned = partner(mine, k)
        peers[k] = (me - digit + plain, plain, turned)
    barrier = enter([peers[k][0] for k in rounds])

    for arrival, first in zip(arrivals, range(0, channels, step)):
        arrival.wait()
        values = fb[first : first + step, :].astype(jnp.float32)
        centre = jnp.mean(values, axis=1, keepdims=True)
        moved = values - centre
        spread = jnp.mean(jnp.square(moved), axis=1, keepdims=True)
        scaled = moved * lax.rsqrt(spread + epsilon)
        for s in range(SUB):
            for m in range(count):
                at = s * wide + m * LANES
                norm[m, pl.ds(first * SUB + s, step, stride=SUB), :] = scaled[:, at : at + LANES]

    partial = None
    for c in range(channels):
        row = [norm[m, c * SUB : (c + 1) * SUB, :] for m in range(count)]
        partial = row if partial is None else plus(partial, row)
    for e in range(ROWS):
        s, m = 2 * (e // count), e % count
        pieces[e] = partial[m][s : s + 2, :]
    if rounds:
        pl.semaphore_wait(barrier, len(rounds))
    scatter = {}
    for k in rounds:
        chan, plain, turned = peers[k]
        scatter[k] = remote(
            pieces.at[pl.ds(plain * held, held)], landed.at[digit], scat_send, scat_recv, k, chan
        )
        scatter[k].start()

    table_in.wait()
    single = table[0]
    for q in range(channels // 4):
        row = []
        for c in range(4):
            at = (4 * q + c) * SUB
            row.append([norm[m, at : at + SUB, :] for m in range(count)])
        low = plus(row[0], advanced(row[1], single))
        high = plus(row[2], advanced(row[3], single))
        merged = plus(low, advanced(high, single))
        for m in range(count):
            base[q, :, m * LANES : (m + 1) * LANES] = merged[m]

    def tiles_of(load):
        return [load(slice(m * LANES, (m + 1) * LANES)) for m in range(count)]

    subs = channels // 4
    view = base.reshape(subs // 2, 2, 1, SUB, wide)
    trials = 1
    for target in (level2, level4, level8, send):
        trials *= 2
        subs //= 2
        for i in range(trials):
            low = tiles_of(lambda w: view[:, 0, i // 2, :, w])
            high = tiles_of(lambda w: view[:, 1, i // 2, :, w])
            merged = plus(low, advanced(high, table[trials - 1 + i]))
            for m in range(count):
                w = slice(m * LANES, (m + 1) * LANES)
                if subs > 1:
                    target[:, i, :, w] = merged[m]
                else:
                    target[i, :, w] = merged[m][0]
        if subs > 1:
            view = target.reshape(subs // 2, 2, trials, SUB, wide)

    copies = {}
    for k in rounds:
        chan, plain, turned = peers[k]
        copies[k] = remote(
            send.at[pl.ds(turned * held, held)], rows.at[pl.ds(digit * held, held)], row_send, row_recv, k, chan
        )
        copies[k].start()
    own = pltpu.make_async_copy(
        send.at[pl.ds(my_turn * held, held)], rows.at[pl.ds(digit * held, held)], own_sem
    )
    own.start()

    total = pieces[pl.ds(digit * held, held)]
    for k in rounds:
        scatter[k].wait_recv()
        total = total + landed[peers[k][1]]
    gathered[pl.ds(digit * held, held)] = total * (1.0 / total_channels)
    gather = {}
    for k in rounds:
        here = gathered.at[pl.ds(digit * held, held)]
        gather[k] = remote(here, here, gath_send, gath_recv, k, peers[k][0])
        gather[k].start()
    for k in rounds:
        gather[k].wait_recv()
    mean = []
    for m in range(count):
        mean.append(jnp.concatenate([gathered[a * count + m] for a in range(SUB // 2)], axis=0))

    for j in range(held):
        trial = my_turn * held + j
        line = plus(mean, advanced(mean, single))
        line = plus(line, advanced(line, single))
        for level in range(1, 5):
            now = trial // (1 << 4 - level)
            line = plus(line, advanced(line, table[(1 << level) - 1 + now]))
        for m in range(count):
            mean_row[j, :, m * LANES : (m + 1) * LANES] = line[m]

    own.wait()
    for k in rounds:
        copies[k].wait_recv()
    for k in rounds:
        scatter[k].wait_send()
        gather[k].wait_send()
        copies[k].wait_send()


def front(filterbank, shift_table, bits, total_channels):
    channels, length = filterbank.shape
    wide = length // SUB
    group = 1 << bits
    held = ROWS // group
    f32 = jnp.float32
    return pl.pallas_call(
        functools.partial(front_kernel, bits, total_channels),
        out_shape=(
            jax.ShapeDtypeStruct((ROWS, SUB, wide), f32),
            jax.ShapeDtypeStruct((held, SUB, wide), f32),
        ),
        in_specs=[pl.BlockSpec(memory_space=pltpu.HBM)] * 2,
        out_specs=(pl.BlockSpec(memory_space=pl.ANY), pl.BlockSpec(memory_space=pltpu.VMEM)),
        scratch_shapes=[
            pltpu.VMEM(filterbank.shape, filterbank.dtype),
            pltpu.SMEM(shift_table.shape, shift_table.dtype),
            pltpu.SemaphoreType.DMA((channels // 16,)),
            pltpu.SemaphoreType.DMA,
            pltpu.VMEM((wide // LANES, channels * SUB, LANES), f32),
            pltpu.VMEM((16, SUB, wide), f32),
            pltpu.VMEM((8, 2, SUB, wide), f32),
            pltpu.VMEM((4, 4, SUB, wide), f32),
            pltpu.VMEM((2, 8, SUB, wide), f32),
            pltpu.VMEM((ROWS, SUB, wide), f32),
            pltpu.VMEM((ROWS, 2, LANES), f32),
            pltpu.VMEM((group, held, 2, LANES), f32),
            pltpu.VMEM((ROWS, 2, LANES), f32),
        ]
        + [pltpu.SemaphoreType.DMA((group,))] * 6
        + [pltpu.SemaphoreType.DMA],
        compiler_params=pltpu.CompilerParams(collective_id=0, has_side_effects=True),
    )(filterbank, shift_table)


def exchange_kernel(bits, stride, block, rows, row_send, row_recv, own_sem):
    group = 1 << bits
    held = ROWS // group
    me = lax.axis_index("chan")
    digit = (me // stride) % group
    mine = digit_bits(digit, bits)
    _, my_turn = partner(mine, 0)
    rounds = peer_rounds(bits)
    peers = {}
    for k in rounds:
        plain, turned = partner(mine, k)
        peers[k] = (me + (plain - digit) * stride, turned)
    barrier = enter([peers[k][0] for k in rounds])
    pl.semaphore_wait(barrier, len(rounds))
    there = rows.at[pl.ds(digit * held, held)]
    copies = {}
    for k in rounds:
        chan, turned = peers[k]
        copies[k] = remote(block.at[pl.ds(turned * held, held)], there, row_send, row_recv, k, chan)
        copies[k].start()
    own = pltpu.make_async_copy(block.at[pl.ds(my_turn * held, held)], there, own_sem)
    own.start()
    own.wait()
    for k in rounds:
        copies[k].wait()


def exchange(block, bits, stride, number):
    group = 1 << bits
    return pl.pallas_call(
        functools.partial(exchange_kernel, bits, stride),
        out_shape=jax.ShapeDtypeStruct(block.shape, block.dtype),
        in_specs=[pl.BlockSpec(memory_space=pltpu.VMEM)],
        out_specs=pl.BlockSpec(memory_space=pl.ANY),
        scratch_shapes=[pltpu.SemaphoreType.DMA((group,))] * 2 + [pltpu.SemaphoreType.DMA],
        compiler_params=pltpu.CompilerParams(
            collective_id=number, has_side_effects=True
        ),
    )(block)


def merge_rows(bits, merged, largest, block, correction, table, place, levels, keep, halves):
    group = 1 << bits
    held = ROWS // group
    wide = block.shape[-1]
    count = wide // LANES
    sub = lax.broadcasted_iota(jnp.int32, (SUB, LANES), 0)

    def put(level, row, tiles, is_upper):
        if level == bits:
            keep(row, tiles)
            return
        for m in range(count):
            levels[level][row, :, m * LANES : (m + 1) * LANES] = tiles[m]
            if is_upper and m * LANES < 2 * (merged * ROWS << level + 1):
                levels[level][row, :, wide + m * LANES : wide + (m + 1) * LANES] = next_sublane(tiles[m])

    def load(base):
        for c in range(ROWS // 2):
            tiles = []
            for m in range(count):
                w = slice(m * LANES, (m + 1) * LANES)
                tile = block[base + c, :, w]
                tiles.append(tile if correction is None else tile - correction[c % held, :, w])
            put(0, base + c, tiles, c // held % 2 == 1)

    def run(level, base, size):
        trials = held << level
        now = 2 * trials
        whole = merged * ROWS << level + 1
        source = levels[level]
        start = 2 * now * place
        at = start % wide // LANES
        pairs = [(q, i) for i in range(now) for q in range(size // now)]
        for first in range(0, size, 8):
            made = []
            for q, i in pairs[first : first + 8]:
                shift = table[whole - 1 + place * now + i]
                low = base + 2 * q * trials + i // 2
                high = low + trials
                tiles = [
                    source[high, :, pl.ds(pl.multiple_of((at + m) * LANES, LANES), LANES)]
                    for m in range(count + 1)
                ]
                moved = combine(tiles, shift & (LANES - 1))
                if largest >= wide:
                    up = jnp.minimum(start // wide, SUB)
                    moved = [
                        jnp.where(sub < SUB - up, pltpu.roll(tile, (SUB - up) & (SUB - 1), 0), 0.0)
                        for tile in moved
                    ]
                lower = [source[low, :, m * LANES : (m + 1) * LANES] for m in range(count)]
                made.append((base + q * now + i, plus(lower, moved), q % 2 == 1 or now == size))
            for row, tiles, is_upper in made:
                put(level + 1, row, tiles, is_upper)

    for base, ready in halves:
        ready()
        load(base)
        for level in range(bits - 1):
            run(level, base, ROWS // 2)
    run(bits - 1, 0, ROWS)


def stage_position(merged, bits):
    me = lax.axis_index("chan")
    known = merged.bit_length() - 1 + bits
    return partner(digit_bits(me, known), 0)[1]


def middle_kernel(bits, merged, largest, corrected, table_far, block, *rest):
    correction = rest[0] if corrected else None
    out, table, table_sem = rest[corrected : corrected + 3]
    levels = rest[corrected + 3 :]
    table_in = pltpu.make_async_copy(table_far, table, table_sem)
    table_in.start()

    def keep(row, tiles):
        for m in range(len(tiles)):
            out[row, :, m * LANES : (m + 1) * LANES] = tiles[m]

    place = stage_position(merged, bits)
    halves = [(0, table_in.wait), (ROWS // 2, lambda: None)]
    merge_rows(bits, merged, largest, block, correction, table, place, levels, keep, halves)


def back_kernel(bits, merged, largest, corrected, table_far, widths_far, block, *rest):
    correction = rest[0] if corrected else None
    dedispersed, peaks, flat, widths, widths_sem, table, table_sem = rest[corrected : corrected + 7]
    levels = rest[corrected + 7 :]
    wide = block.shape[-1]
    length = wide * SUB
    table_in = pltpu.make_async_copy(table_far, table, table_sem)
    widths_in = pltpu.make_async_copy(widths_far, widths, widths_sem)
    table_in.start()
    widths_in.start()

    def keep(row, tiles):
        for m in range(len(tiles)):
            flat[m, row * SUB : (row + 1) * SUB, :] = tiles[m]

    place = stage_position(merged, bits)
    halves = [(0, table_in.wait), (ROWS // 2, lambda: None)]
    merge_rows(bits, merged, largest, block, correction, table, place, levels, keep, halves)
    finish(length, flat, widths_in, widths, dedispersed, peaks)


def finish(length, flat, widths_in, widths, dedispersed, peaks):
    wide = length // SUB
    series = [
        jnp.concatenate([flat[m, pl.ds(s, ROWS, stride=SUB), :] for m in range(wide // LANES)], axis=1)
        for s in range(SUB)
    ]
    summed = series[0]
    for part in series[1:]:
        summed = summed + part
    centre = jnp.sum(summed, axis=1, keepdims=True) * (1.0 / length)
    series = [part - centre for part in series]
    squared = jnp.square(series[0])
    for part in series[1:]:
        squared = squared + jnp.square(part)
    spread = jnp.sum(squared, axis=1, keepdims=True) * (1.0 / length)
    factor = lax.rsqrt(spread + epsilon)
    series = [part * factor for part in series]
    for s in range(SUB):
        dedispersed[:, s * wide : (s + 1) * wide] = series[s].astype(jnp.bfloat16)

    piece = 2 * LANES
    stacked = jnp.concatenate(
        [part[:, a : a + piece] for part in series for a in range(0, wide, piece)], axis=0
    )
    triangle = jnp.where(
        lax.broadcasted_iota(jnp.int32, (piece, piece + LANES), 0)
        <= lax.broadcasted_iota(jnp.int32, (piece, piece + LANES), 1),
        1.0,
        0.0,
    ).astype(jnp.bfloat16)
    rest_value = stacked
    inner = None
    for _ in range(3):
        top = rest_value.astype(jnp.bfloat16)
        rest_value = rest_value - top.astype(jnp.float32)
        product = jnp.dot(top, triangle, preferred_element_type=jnp.float32)
        inner = product if inner is None else inner + product
    offset = jnp.zeros((ROWS, LANES), jnp.float32)
    prefix = []
    for p in range(length // piece):
        one = inner[p * ROWS : (p + 1) * ROWS, :]
        prefix += [one[:, :LANES] + offset, one[:, LANES:piece] + offset]
        offset = offset + one[:, piece:]

    lane = lax.broadcasted_iota(jnp.int32, (ROWS, LANES), 1)
    diagonal = lane == lax.broadcasted_iota(jnp.int32, (ROWS, LANES), 0)
    zero = jnp.zeros((ROWS, LANES), jnp.float32)
    count = peaks.shape[0]
    widths_in.wait()
    for i in range(count):
        width = widths[i]
        whole, amount = divmod(1 << i, LANES)
        amount = width - whole * LANES
        keep = lane >= amount
        best = None
        before = zero
        for c in range(len(prefix)):
            source = c - whole
            now = pltpu.roll(prefix[source], amount, 1) if source >= 0 else zero
            box = prefix[c] - jnp.where(keep, now, before)
            before = now
            best = box if best is None else jnp.maximum(best, box)
        root = lax.rsqrt(jnp.full((ROWS, 1), width, jnp.int32).astype(jnp.float32))
        column = jnp.max(best, axis=1, keepdims=True) * root
        line = jnp.sum(jnp.where(diagonal, column, 0.0), axis=0, keepdims=True)
        peaks[i : i + 1, :] = line[:, :ROWS]


def merge(block, correction, shift_table, bits, merged, box_widths):
    wide = block.shape[-1]
    largest = 2 * ((merged * ROWS << bits) - 1) + 1
    corrected = correction is not None
    far = pl.BlockSpec(memory_space=pltpu.HBM)
    vmem = pl.BlockSpec(memory_space=pltpu.VMEM)
    levels = [pltpu.VMEM((ROWS, SUB, 2 * wide), jnp.float32)] * bits
    table = [pltpu.SMEM(shift_table.shape, shift_table.dtype), pltpu.SemaphoreType.DMA]
    params = pltpu.CompilerParams()
    data = (block, correction) if corrected else (block,)
    if box_widths is None:
        return pl.pallas_call(
            functools.partial(middle_kernel, bits, merged, largest, corrected),
            out_shape=jax.ShapeDtypeStruct(block.shape, jnp.float32),
            in_specs=[far] + [vmem] * len(data),
            out_specs=vmem,
            scratch_shapes=table + levels,
            compiler_params=params,
        )(shift_table, *data)
    widths = [pltpu.SMEM(box_widths.shape, box_widths.dtype), pltpu.SemaphoreType.DMA]
    return pl.pallas_call(
        functools.partial(back_kernel, bits, merged, largest, corrected),
        out_shape=(
            jax.ShapeDtypeStruct((ROWS, SUB * wide), jnp.bfloat16),
            jax.ShapeDtypeStruct((box_widths.shape[0], ROWS), jnp.float32),
        ),
        in_specs=[far] * 2 + [vmem] * len(data),
        out_specs=(vmem, vmem),
        scratch_shapes=[pltpu.VMEM((wide // LANES, ROWS * SUB, LANES), jnp.float32)] + widths + table + levels,
        compiler_params=params,
    )(shift_table, box_widths, *data)


def shards(filterbank, shift_table, box_widths):
    devices = lax.axis_size("chan")
    all_bits = devices.bit_length() - 1
    bits = min(GROUP_BITS, all_bits)
    rows, correction = front(filterbank, shift_table, bits, filterbank.shape[0] * devices)
    for bit in range(bits, all_bits):
        route = [(source, source ^ 1 << bit) for source in range(devices)]
        correction = correction + lax.ppermute(correction, "chan", route)
    done = 0
    while True:
        last = done + bits == all_bits
        result = merge(rows, correction, shift_table, bits, 1 << done, box_widths if last else None)
        if last:
            return result
        done += bits
        bits = min(GROUP_BITS, all_bits - done)
        rows = exchange(result, bits, 1 << done, done)
        correction = None


def solution(mesh):
    placed = (P(("beam", "chan"), None), P(), P())
    return jax.shard_map(
        shards,
        mesh=mesh,
        in_specs=placed,
        out_specs=(P(("beam", "chan"), None), P("beam", "chan")),
        check_vma=False,
    )
```

```python
import functools

import jax
import jax.numpy as jnp
from jax import lax
from jax.experimental import pallas as pl
from jax.experimental.pallas import tpu as pltpu
from jax.sharding import PartitionSpec as P

ROWS = 16
SUB = 8
LANES = 128
GROUP_BITS = 4

epsilon = 1e-05


def lane_index():
    return lax.broadcasted_iota(jnp.int32, (SUB, LANES), 1)


def next_sublane(tile):
    sub = lax.broadcasted_iota(jnp.int32, tile.shape, tile.ndim - 2)
    return jnp.where(sub == SUB - 1, 0.0, pltpu.roll(tile, SUB - 1, tile.ndim - 2))


def combine(tiles, amount):
    back = (LANES - amount) & (LANES - 1)
    turned = [pltpu.roll(tile, back, tile.ndim - 1) for tile in tiles]
    lane = lax.broadcasted_iota(jnp.int32, tiles[0].shape, tiles[0].ndim - 1)
    keep = lane < LANES - amount
    return [jnp.where(keep, turned[i], turned[i + 1]) for i in range(len(tiles) - 1)]


def advanced(tiles, amount):
    return combine(list(tiles) + [next_sublane(tiles[0])], amount)


def plus(first, second):
    return [a + b for a, b in zip(first, second)]


def digit_bits(digit, bits):
    return [(digit // (1 << i)) % 2 for i in range(bits)]


def partner(bit_values, k):
    flipped = [1 - b if k >> i & 1 else b for i, b in enumerate(bit_values)]
    plain = sum((b * (1 << i) for i, b in enumerate(flipped)), 0)
    turned = sum((b * (1 << len(flipped) - 1 - i) for i, b in enumerate(flipped)), 0)
    return plain, turned


def peer_rounds(bits):
    return sorted(range(1, 1 << bits), reverse=True)


def enter(peers):
    barrier = pltpu.get_barrier_semaphore()
    for peer in peers:
        pl.semaphore_signal(
            barrier, inc=1, device_id={"chan": peer}, device_id_type=pl.DeviceIdType.MESH
        )
    return barrier


def remote(src, dst, send_sem, recv_sem, k, peer):
    return pltpu.make_async_remote_copy(
        src_ref=src,
        dst_ref=dst,
        send_sem=send_sem.at[k],
        recv_sem=recv_sem.at[k],
        device_id={"chan": peer},
        device_id_type=pl.DeviceIdType.MESH,
    )


def front_kernel(
    bits, total_channels, fb_far, table_far, rows, mean_far,
    mean_row, mean_sem,
    fb, table, in_sem, table_sem, norm, base, level2, level4, level8, send, pieces, landed, gathered,
    scat_send, scat_recv, gath_send, gath_recv, row_send, row_recv, own_sem,
):
    group = 1 << bits
    held = ROWS // group
    channels, length = fb.shape
    wide = length // SUB
    count = wide // LANES
    step = 16
    arrivals = []
    for n, first in enumerate(range(0, channels, step)):
        block = pl.ds(first, step)
        arrivals.append(pltpu.make_async_copy(fb_far.at[block], fb.at[block], in_sem.at[n]))
    table_in = pltpu.make_async_copy(table_far, table, table_sem)
    for arrival in arrivals:
        arrival.start()
    table_in.start()
    me = lax.axis_index("chan")
    digit = me % group
    mine = digit_bits(digit, bits)
    _, my_turn = partner(mine, 0)
    rounds = peer_rounds(bits)
    peers = {}
    for k in rounds:
        plain, turned = partner(mine, k)
        peers[k] = (me - digit + plain, plain, turned)
    barrier = enter([peers[k][0] for k in rounds])

    for arrival, first in zip(arrivals, range(0, channels, step)):
        arrival.wait()
        values = fb[first : first + step, :].astype(jnp.float32)
        centre = jnp.mean(values, axis=1, keepdims=True)
        moved = values - centre
        spread = jnp.mean(jnp.square(moved), axis=1, keepdims=True)
        scaled = moved * lax.rsqrt(spread + epsilon)
        for s in range(SUB):
            for m in range(count):
                at = s * wide + m * LANES
                norm[m, pl.ds(first * SUB + s, step, stride=SUB), :] = scaled[:, at : at + LANES]

    partial = None
    for c in range(channels):
        row = [norm[m, c * SUB : (c + 1) * SUB, :] for m in range(count)]
        partial = row if partial is None else plus(partial, row)
    for e in range(ROWS):
        s, m = 2 * (e // count), e % count
        pieces[e] = partial[m][s : s + 2, :]
    if rounds:
        pl.semaphore_wait(barrier, len(rounds))
    scatter = {}
    for k in rounds:
        chan, plain, turned = peers[k]
        scatter[k] = remote(
            pieces.at[pl.ds(plain * held, held)], landed.at[digit], scat_send, scat_recv, k, chan
        )
        scatter[k].start()

    table_in.wait()
    single = table[0]
    for q in range(channels // 4):
        row = []
        for c in range(4):
            at = (4 * q + c) * SUB
            row.append([norm[m, at : at + SUB, :] for m in range(count)])
        low = plus(row[0], advanced(row[1], single))
        high = plus(row[2], advanced(row[3], single))
        merged = plus(low, advanced(high, single))
        for m in range(count):
            base[q, :, m * LANES : (m + 1) * LANES] = merged[m]

    def tiles_of(load):
        return [load(slice(m * LANES, (m + 1) * LANES)) for m in range(count)]

    subs = channels // 4
    view = base.reshape(subs // 2, 2, 1, SUB, wide)
    trials = 1
    for target in (level2, level4, level8, send):
        trials *= 2
        subs //= 2
        for i in range(trials):
            low = tiles_of(lambda w: view[:, 0, i // 2, :, w])
            high = tiles_of(lambda w: view[:, 1, i // 2, :, w])
            merged = plus(low, advanced(high, table[trials - 1 + i]))
            for m in range(count):
                w = slice(m * LANES, (m + 1) * LANES)
                if subs > 1:
                    target[:, i, :, w] = merged[m]
                else:
                    target[i, :, w] = merged[m][0]
        if subs > 1:
            view = target.reshape(subs // 2, 2, trials, SUB, wide)

    copies = {}
    for k in rounds:
        chan, plain, turned = peers[k]
        copies[k] = remote(
            send.at[pl.ds(turned * held, held)], rows.at[pl.ds(digit * held, held)], row_send, row_recv, k, chan
        )
        copies[k].start()
    own = pltpu.make_async_copy(
        send.at[pl.ds(my_turn * held, held)], rows.at[pl.ds(digit * held, held)], own_sem
    )
    own.start()

    total = pieces[pl.ds(digit * held, held)]
    for k in rounds:
        scatter[k].wait_recv()
        total = total + landed[peers[k][1]]
    gathered[pl.ds(digit * held, held)] = total * (1.0 / total_channels)
    gather = {}
    for k in rounds:
        here = gathered.at[pl.ds(digit * held, held)]
        gather[k] = remote(here, here, gath_send, gath_recv, k, peers[k][0])
        gather[k].start()
    for k in rounds:
        gather[k].wait_recv()
    mean = []
    for m in range(count):
        mean.append(jnp.concatenate([gathered[a * count + m] for a in range(SUB // 2)], axis=0))

    for j in range(held):
        trial = my_turn * held + j
        line = plus(mean, advanced(mean, single))
        line = plus(line, advanced(line, single))
        for level in range(1, 5):
            now = trial // (1 << 4 - level)
            line = plus(line, advanced(line, table[(1 << level) - 1 + now]))
        for m in range(count):
            mean_row[j, :, m * LANES : (m + 1) * LANES] = line[m]

    mean_out = pltpu.make_async_copy(mean_row, mean_far, mean_sem)
    mean_out.start()
    own.wait()
    for k in rounds:
        copies[k].wait_recv()
    mean_out.wait()
    for k in rounds:
        scatter[k].wait_send()
        gather[k].wait_send()
        copies[k].wait_send()


def front(filterbank, shift_table, bits, total_channels):
    channels, length = filterbank.shape
    wide = length // SUB
    group = 1 << bits
    held = ROWS // group
    f32 = jnp.float32
    return pl.pallas_call(
        functools.partial(front_kernel, bits, total_channels),
        out_shape=(
            jax.ShapeDtypeStruct((ROWS, SUB, wide), f32),
            jax.ShapeDtypeStruct((held, SUB, wide), f32),
        ),
        in_specs=[pl.BlockSpec(memory_space=pltpu.HBM)] * 2,
        out_specs=(pl.BlockSpec(memory_space=pl.ANY),) * 2,
        scratch_shapes=[
            pltpu.VMEM((held, SUB, wide), f32),
            pltpu.SemaphoreType.DMA,
            pltpu.VMEM(filterbank.shape, filterbank.dtype),
            pltpu.SMEM(shift_table.shape, shift_table.dtype),
            pltpu.SemaphoreType.DMA((channels // 16,)),
            pltpu.SemaphoreType.DMA,
            pltpu.VMEM((wide // LANES, channels * SUB, LANES), f32),
            pltpu.VMEM((16, SUB, wide), f32),
            pltpu.VMEM((8, 2, SUB, wide), f32),
            pltpu.VMEM((4, 4, SUB, wide), f32),
            pltpu.VMEM((2, 8, SUB, wide), f32),
            pltpu.VMEM((ROWS, SUB, wide), f32),
            pltpu.VMEM((ROWS, 2, LANES), f32),
            pltpu.VMEM((group, held, 2, LANES), f32),
            pltpu.VMEM((ROWS, 2, LANES), f32),
        ]
        + [pltpu.SemaphoreType.DMA((group,))] * 6
        + [pltpu.SemaphoreType.DMA],
        compiler_params=pltpu.CompilerParams(collective_id=0, has_side_effects=True),
    )(filterbank, shift_table)


def exchange_kernel(bits, stride, block, rows, row_send, row_recv, own_sem):
    group = 1 << bits
    held = ROWS // group
    me = lax.axis_index("chan")
    digit = (me // stride) % group
    mine = digit_bits(digit, bits)
    _, my_turn = partner(mine, 0)
    rounds = peer_rounds(bits)
    peers = {}
    for k in rounds:
        plain, turned = partner(mine, k)
        peers[k] = (me + (plain - digit) * stride, turned)
    barrier = enter([peers[k][0] for k in rounds])
    pl.semaphore_wait(barrier, len(rounds))
    there = rows.at[pl.ds(digit * held, held)]
    copies = {}
    for k in rounds:
        chan, turned = peers[k]
        copies[k] = remote(block.at[pl.ds(turned * held, held)], there, row_send, row_recv, k, chan)
        copies[k].start()
    own = pltpu.make_async_copy(block.at[pl.ds(my_turn * held, held)], there, own_sem)
    own.start()
    own.wait()
    for k in rounds:
        copies[k].wait()


def exchange(block, bits, stride, number):
    group = 1 << bits
    return pl.pallas_call(
        functools.partial(exchange_kernel, bits, stride),
        out_shape=jax.ShapeDtypeStruct(block.shape, block.dtype),
        in_specs=[pl.BlockSpec(memory_space=pltpu.VMEM)],
        out_specs=pl.BlockSpec(memory_space=pl.ANY),
        scratch_shapes=[pltpu.SemaphoreType.DMA((group,))] * 2 + [pltpu.SemaphoreType.DMA],
        compiler_params=pltpu.CompilerParams(
            collective_id=number, has_side_effects=True
        ),
    )(block)


def merge_rows(bits, merged, largest, block, correction, table, place, levels, keep, halves):
    group = 1 << bits
    held = ROWS // group
    wide = block.shape[-1]
    count = wide // LANES
    sub = lax.broadcasted_iota(jnp.int32, (SUB, LANES), 0)

    def put(level, row, tiles, is_upper):
        if level == bits:
            keep(row, tiles)
            return
        for m in range(count):
            levels[level][row, :, m * LANES : (m + 1) * LANES] = tiles[m]
            if is_upper and m * LANES < 2 * (merged * ROWS << level + 1):
                levels[level][row, :, wide + m * LANES : wide + (m + 1) * LANES] = next_sublane(tiles[m])

    def load(base):
        for c in range(ROWS // 2):
            tiles = []
            for m in range(count):
                w = slice(m * LANES, (m + 1) * LANES)
                tile = block[base + c, :, w]
                tiles.append(tile if correction is None else tile - correction[c % held, :, w])
            put(0, base + c, tiles, c // held % 2 == 1)

    def run(level, base, size):
        trials = held << level
        now = 2 * trials
        whole = merged * ROWS << level + 1
        source = levels[level]
        start = 2 * now * place
        at = start % wide // LANES
        pairs = [(q, i) for i in range(now) for q in range(size // now)]
        for first in range(0, size, 8):
            made = []
            for q, i in pairs[first : first + 8]:
                shift = table[whole - 1 + place * now + i]
                low = base + 2 * q * trials + i // 2
                high = low + trials
                tiles = [
                    source[high, :, pl.ds(pl.multiple_of((at + m) * LANES, LANES), LANES)]
                    for m in range(count + 1)
                ]
                moved = combine(tiles, shift & (LANES - 1))
                if largest >= wide:
                    up = jnp.minimum(start // wide, SUB)
                    moved = [
                        jnp.where(sub < SUB - up, pltpu.roll(tile, (SUB - up) & (SUB - 1), 0), 0.0)
                        for tile in moved
                    ]
                lower = [source[low, :, m * LANES : (m + 1) * LANES] for m in range(count)]
                made.append((base + q * now + i, plus(lower, moved), q % 2 == 1 or now == size))
            for row, tiles, is_upper in made:
                put(level + 1, row, tiles, is_upper)

    for base, ready in halves:
        ready()
        load(base)
        for level in range(bits - 1):
            run(level, base, ROWS // 2)
    run(bits - 1, 0, ROWS)


def stage_position(merged, bits):
    me = lax.axis_index("chan")
    known = merged.bit_length() - 1 + bits
    return partner(digit_bits(me, known), 0)[1]


def middle_kernel(bits, merged, largest, corrected, table_far, block, *rest):
    correction = rest[0] if corrected else None
    out, table, table_sem = rest[corrected : corrected + 3]
    levels = rest[corrected + 3 :]
    table_in = pltpu.make_async_copy(table_far, table, table_sem)
    table_in.start()

    def keep(row, tiles):
        for m in range(len(tiles)):
            out[row, :, m * LANES : (m + 1) * LANES] = tiles[m]

    place = stage_position(merged, bits)
    halves = [(0, table_in.wait), (ROWS // 2, lambda: None)]
    merge_rows(bits, merged, largest, block, correction, table, place, levels, keep, halves)


def back_kernel(bits, merged, largest, corrected, table_far, widths_far, block_far, *rest):
    dedispersed_far, peaks, flat, widths, widths_sem, table, table_sem = rest[corrected : corrected + 7]
    block, block_sem, dedispersed, dedispersed_sem, *levels = rest[corrected + 7 :]
    halves_in = []
    for n in range(2):
        part = pl.ds(n * (ROWS // 2), ROWS // 2)
        halves_in.append(pltpu.make_async_copy(block_far.at[part], block.at[part], block_sem.at[n]))
        halves_in[n].start()
    correction = None
    if corrected:
        correction, correction_sem, *levels = levels
        correction_in = pltpu.make_async_copy(rest[0], correction, correction_sem)
        correction_in.start()
    wide = block.shape[-1]
    length = wide * SUB
    table_in = pltpu.make_async_copy(table_far, table, table_sem)
    widths_in = pltpu.make_async_copy(widths_far, widths, widths_sem)
    table_in.start()
    widths_in.start()

    def keep(row, tiles):
        for m in range(len(tiles)):
            flat[m, row * SUB : (row + 1) * SUB, :] = tiles[m]

    place = stage_position(merged, bits)

    def first():
        halves_in[0].wait()
        if corrected:
            correction_in.wait()
        table_in.wait()

    halves = [(0, first), (ROWS // 2, halves_in[1].wait)]
    merge_rows(bits, merged, largest, block, correction, table, place, levels, keep, halves)
    dedispersed_out = pltpu.make_async_copy(dedispersed, dedispersed_far, dedispersed_sem)
    finish(length, flat, widths_in, widths, dedispersed, dedispersed_out, peaks)
    dedispersed_out.wait()


def finish(length, flat, widths_in, widths, dedispersed, dedispersed_out, peaks):
    wide = length // SUB
    series = [
        jnp.concatenate([flat[m, pl.ds(s, ROWS, stride=SUB), :] for m in range(wide // LANES)], axis=1)
        for s in range(SUB)
    ]
    summed = series[0]
    for part in series[1:]:
        summed = summed + part
    centre = jnp.sum(summed, axis=1, keepdims=True) * (1.0 / length)
    series = [part - centre for part in series]
    squared = jnp.square(series[0])
    for part in series[1:]:
        squared = squared + jnp.square(part)
    spread = jnp.sum(squared, axis=1, keepdims=True) * (1.0 / length)
    factor = lax.rsqrt(spread + epsilon)
    series = [part * factor for part in series]
    for s in range(SUB):
        dedispersed[:, s * wide : (s + 1) * wide] = series[s].astype(jnp.bfloat16)
    dedispersed_out.start()

    piece = 2 * LANES
    stacked = jnp.concatenate(
        [part[:, a : a + piece] for part in series for a in range(0, wide, piece)], axis=0
    )
    triangle = jnp.where(
        lax.broadcasted_iota(jnp.int32, (piece, piece + LANES), 0)
        <= lax.broadcasted_iota(jnp.int32, (piece, piece + LANES), 1),
        1.0,
        0.0,
    ).astype(jnp.bfloat16)
    rest_value = stacked
    inner = None
    for _ in range(3):
        top = rest_value.astype(jnp.bfloat16)
        rest_value = rest_value - top.astype(jnp.float32)
        product = jnp.dot(top, triangle, preferred_element_type=jnp.float32)
        inner = product if inner is None else inner + product
    offset = jnp.zeros((ROWS, LANES), jnp.float32)
    prefix = []
    for p in range(length // piece):
        one = inner[p * ROWS : (p + 1) * ROWS, :]
        prefix += [one[:, :LANES] + offset, one[:, LANES:piece] + offset]
        offset = offset + one[:, piece:]

    lane = lax.broadcasted_iota(jnp.int32, (ROWS, LANES), 1)
    diagonal = lane == lax.broadcasted_iota(jnp.int32, (ROWS, LANES), 0)
    zero = jnp.zeros((ROWS, LANES), jnp.float32)
    count = peaks.shape[0]
    widths_in.wait()
    for i in range(count):
        width = widths[i]
        whole, amount = divmod(1 << i, LANES)
        amount = width - whole * LANES
        keep = lane >= amount
        best = None
        before = zero
        for c in range(len(prefix)):
            source = c - whole
            now = pltpu.roll(prefix[source], amount, 1) if source >= 0 else zero
            box = prefix[c] - jnp.where(keep, now, before)
            before = now
            best = box if best is None else jnp.maximum(best, box)
        root = lax.rsqrt(jnp.full((ROWS, 1), width, jnp.int32).astype(jnp.float32))
        column = jnp.max(best, axis=1, keepdims=True) * root
        line = jnp.sum(jnp.where(diagonal, column, 0.0), axis=0, keepdims=True)
        peaks[i : i + 1, :] = line[:, :ROWS]


def merge(block, correction, shift_table, bits, merged, box_widths):
    wide = block.shape[-1]
    largest = 2 * ((merged * ROWS << bits) - 1) + 1
    corrected = correction is not None
    far = pl.BlockSpec(memory_space=pltpu.HBM)
    vmem = pl.BlockSpec(memory_space=pltpu.VMEM)
    levels = [pltpu.VMEM((ROWS, SUB, 2 * wide), jnp.float32)] * bits
    table = [pltpu.SMEM(shift_table.shape, shift_table.dtype), pltpu.SemaphoreType.DMA]
    params = pltpu.CompilerParams()
    data = (block, correction) if corrected else (block,)
    if box_widths is None:
        return pl.pallas_call(
            functools.partial(middle_kernel, bits, merged, largest, corrected),
            out_shape=jax.ShapeDtypeStruct(block.shape, jnp.float32),
            in_specs=[far] + [vmem] * len(data),
            out_specs=vmem,
            scratch_shapes=table + levels,
            compiler_params=params,
        )(shift_table, *data)
    widths = [pltpu.SMEM(box_widths.shape, box_widths.dtype), pltpu.SemaphoreType.DMA]
    staged = [
        pltpu.VMEM(block.shape, block.dtype),
        pltpu.SemaphoreType.DMA((2,)),
        pltpu.VMEM((ROWS, SUB * wide), jnp.bfloat16),
        pltpu.SemaphoreType.DMA,
    ]
    if corrected:
        staged += [pltpu.VMEM(correction.shape, correction.dtype), pltpu.SemaphoreType.DMA]
    return pl.pallas_call(
        functools.partial(back_kernel, bits, merged, largest, corrected),
        out_shape=(
            jax.ShapeDtypeStruct((ROWS, SUB * wide), jnp.bfloat16),
            jax.ShapeDtypeStruct((box_widths.shape[0], ROWS), jnp.float32),
        ),
        in_specs=[far] * (2 + len(data)),
        out_specs=(pl.BlockSpec(memory_space=pl.ANY), vmem),
        scratch_shapes=[pltpu.VMEM((wide // LANES, ROWS * SUB, LANES), jnp.float32)] + widths + table + staged + levels,
        compiler_params=params,
    )(shift_table, box_widths, *data)


def shards(filterbank, shift_table, box_widths):
    devices = lax.axis_size("chan")
    all_bits = devices.bit_length() - 1
    bits = min(GROUP_BITS, all_bits)
    rows, correction = front(filterbank, shift_table, bits, filterbank.shape[0] * devices)
    for bit in range(bits, all_bits):
        route = [(source, source ^ 1 << bit) for source in range(devices)]
        correction = correction + lax.ppermute(correction, "chan", route)
    done = 0
    while True:
        last = done + bits == all_bits
        result = merge(rows, correction, shift_table, bits, 1 << done, box_widths if last else None)
        if last:
            return result
        done += bits
        bits = min(GROUP_BITS, all_bits - done)
        rows = exchange(result, bits, 1 << done, done)
        correction = None


def solution(mesh):
    placed = (P(("beam", "chan"), None), P(), P())
    return jax.shard_map(
        shards,
        mesh=mesh,
        in_specs=placed,
        out_specs=(P(("beam", "chan"), None), P("beam", "chan")),
        check_vma=False,
    )
```

```python
import functools

import jax
import jax.numpy as jnp
from jax import lax
from jax.experimental import pallas as pl
from jax.experimental.pallas import tpu as pltpu
from jax.sharding import PartitionSpec as P

ROWS = 16
SUB = 8
LANES = 128
GROUP_BITS = 4

epsilon = 1e-05


def lane_index():
    return lax.broadcasted_iota(jnp.int32, (SUB, LANES), 1)


def next_sublane(tile):
    sub = lax.broadcasted_iota(jnp.int32, tile.shape, tile.ndim - 2)
    return jnp.where(sub == SUB - 1, 0.0, pltpu.roll(tile, SUB - 1, tile.ndim - 2))


def combine(tiles, amount):
    back = (LANES - amount) & (LANES - 1)
    turned = [pltpu.roll(tile, back, tile.ndim - 1) for tile in tiles]
    lane = lax.broadcasted_iota(jnp.int32, tiles[0].shape, tiles[0].ndim - 1)
    keep = lane < LANES - amount
    return [jnp.where(keep, turned[i], turned[i + 1]) for i in range(len(tiles) - 1)]


def advanced(tiles, amount):
    return combine(list(tiles) + [next_sublane(tiles[0])], amount)


def plus(first, second):
    return [a + b for a, b in zip(first, second)]


def digit_bits(digit, bits):
    return [(digit // (1 << i)) % 2 for i in range(bits)]


def partner(bit_values, k):
    flipped = [1 - b if k >> i & 1 else b for i, b in enumerate(bit_values)]
    plain = sum((b * (1 << i) for i, b in enumerate(flipped)), 0)
    turned = sum((b * (1 << len(flipped) - 1 - i) for i, b in enumerate(flipped)), 0)
    return plain, turned


def peer_rounds(bits):
    return sorted(range(1, 1 << bits), reverse=True)


def enter(peers):
    barrier = pltpu.get_barrier_semaphore()
    for peer in peers:
        pl.semaphore_signal(
            barrier, inc=1, device_id={"chan": peer}, device_id_type=pl.DeviceIdType.MESH
        )
    return barrier


def remote(src, dst, send_sem, recv_sem, k, peer):
    return pltpu.make_async_remote_copy(
        src_ref=src,
        dst_ref=dst,
        send_sem=send_sem.at[k],
        recv_sem=recv_sem.at[k],
        device_id={"chan": peer},
        device_id_type=pl.DeviceIdType.MESH,
    )


def front_kernel(
    bits, total_channels, fb_far, table_far, rows, mean_far,
    mean_row, mean_sem,
    fb, table, in_sem, table_sem, norm, base, level2, level4, level8, send, pieces, landed, gathered,
    scat_send, scat_recv, gath_send, gath_recv, row_send, row_recv, own_sem,
):
    group = 1 << bits
    held = ROWS // group
    channels, length = fb.shape
    wide = length // SUB
    count = wide // LANES
    step = 16
    arrivals = []
    for n, first in enumerate(range(0, channels, step)):
        block = pl.ds(first, step)
        arrivals.append(pltpu.make_async_copy(fb_far.at[block], fb.at[block], in_sem.at[n]))
    table_in = pltpu.make_async_copy(table_far, table, table_sem)
    for arrival in arrivals:
        arrival.start()
    table_in.start()
    me = lax.axis_index("chan")
    digit = me % group
    mine = digit_bits(digit, bits)
    _, my_turn = partner(mine, 0)
    rounds = peer_rounds(bits)
    peers = {}
    for k in rounds:
        plain, turned = partner(mine, k)
        peers[k] = (me - digit + plain, plain, turned)
    barrier = enter([peers[k][0] for k in rounds])

    for arrival, first in zip(arrivals, range(0, channels, step)):
        arrival.wait()
        values = fb[first : first + step, :].astype(jnp.float32)
        centre = jnp.mean(values, axis=1, keepdims=True)
        moved = values - centre
        spread = jnp.mean(jnp.square(moved), axis=1, keepdims=True)
        scaled = moved * lax.rsqrt(spread + epsilon)
        for s in range(SUB):
            for m in range(count):
                at = s * wide + m * LANES
                norm[m, pl.ds(first * SUB + s, step, stride=SUB), :] = scaled[:, at : at + LANES]

    partial = None
    for c in range(channels):
        row = [norm[m, c * SUB : (c + 1) * SUB, :] for m in range(count)]
        partial = row if partial is None else plus(partial, row)
    for e in range(ROWS):
        s, m = 2 * (e // count), e % count
        pieces[e] = partial[m][s : s + 2, :]
    if rounds:
        pl.semaphore_wait(barrier, len(rounds))
    scatter = {}
    for k in rounds:
        chan, plain, turned = peers[k]
        scatter[k] = remote(
            pieces.at[pl.ds(plain * held, held)], landed.at[digit], scat_send, scat_recv, k, chan
        )
        scatter[k].start()

    table_in.wait()
    single = table[0]
    for q in range(channels // 4):
        row = []
        for c in range(4):
            at = (4 * q + c) * SUB
            row.append([norm[m, at : at + SUB, :] for m in range(count)])
        low = plus(row[0], advanced(row[1], single))
        high = plus(row[2], advanced(row[3], single))
        merged = plus(low, advanced(high, single))
        for m in range(count):
            base[q, :, m * LANES : (m + 1) * LANES] = merged[m]

    def tiles_of(load):
        return [load(slice(m * LANES, (m + 1) * LANES)) for m in range(count)]

    subs = channels // 4
    view = base.reshape(subs // 2, 2, 1, SUB, wide)
    trials = 1
    for target in (level2, level4, level8):
        trials *= 2
        subs //= 2
        for i in range(trials):
            low = tiles_of(lambda w: view[:, 0, i // 2, :, w])
            high = tiles_of(lambda w: view[:, 1, i // 2, :, w])
            merged = plus(low, advanced(high, table[trials - 1 + i]))
            for m in range(count):
                w = slice(m * LANES, (m + 1) * LANES)
                target[:, i, :, w] = merged[m]
        view = target.reshape(subs // 2, 2, trials, SUB, wide)

    copies = {}
    top = mine[bits - 1]
    for distant, turn in ((True, 1 - top), (False, top)):
        for a in range(group // 2):
            for b in range(held):
                trial = (2 * a + turn) * held + b
                parent = a if held == 1 else trial // 2
                low = tiles_of(lambda w: level8[0, parent, :, w])
                high = tiles_of(lambda w: level8[1, parent, :, w])
                merged = plus(low, advanced(high, table[ROWS - 1 + trial]))
                for m in range(count):
                    send[trial, :, m * LANES : (m + 1) * LANES] = merged[m]
        for k in rounds:
            if (k >= group // 2) == distant:
                chan, plain, turned = peers[k]
                copies[k] = remote(
                    send.at[pl.ds(turned * held, held)], rows.at[pl.ds(digit * held, held)],
                    row_send, row_recv, k, chan,
                )
                copies[k].start()
    own = pltpu.make_async_copy(
        send.at[pl.ds(my_turn * held, held)], rows.at[pl.ds(digit * held, held)], own_sem
    )
    own.start()

    total = pieces[pl.ds(digit * held, held)]
    for k in rounds:
        scatter[k].wait_recv()
        total = total + landed[peers[k][1]]
    gathered[pl.ds(digit * held, held)] = total * (1.0 / total_channels)
    gather = {}
    for k in rounds:
        here = gathered.at[pl.ds(digit * held, held)]
        gather[k] = remote(here, here, gath_send, gath_recv, k, peers[k][0])
        gather[k].start()
    for k in rounds:
        gather[k].wait_recv()
    mean = []
    for m in range(count):
        mean.append(jnp.concatenate([gathered[a * count + m] for a in range(SUB // 2)], axis=0))

    for j in range(held):
        trial = my_turn * held + j
        line = plus(mean, advanced(mean, single))
        line = plus(line, advanced(line, single))
        for level in range(1, 5):
            now = trial // (1 << 4 - level)
            line = plus(line, advanced(line, table[(1 << level) - 1 + now]))
        for m in range(count):
            mean_row[j, :, m * LANES : (m + 1) * LANES] = line[m]

    mean_out = pltpu.make_async_copy(mean_row, mean_far, mean_sem)
    mean_out.start()
    own.wait()
    for k in rounds:
        copies[k].wait_recv()
    mean_out.wait()
    for k in rounds:
        scatter[k].wait_send()
        gather[k].wait_send()
        copies[k].wait_send()


def front(filterbank, shift_table, bits, total_channels):
    channels, length = filterbank.shape
    wide = length // SUB
    group = 1 << bits
    held = ROWS // group
    f32 = jnp.float32
    return pl.pallas_call(
        functools.partial(front_kernel, bits, total_channels),
        out_shape=(
            jax.ShapeDtypeStruct((ROWS, SUB, wide), f32),
            jax.ShapeDtypeStruct((held, SUB, wide), f32),
        ),
        in_specs=[pl.BlockSpec(memory_space=pltpu.HBM)] * 2,
        out_specs=(pl.BlockSpec(memory_space=pl.ANY),) * 2,
        scratch_shapes=[
            pltpu.VMEM((held, SUB, wide), f32),
            pltpu.SemaphoreType.DMA,
            pltpu.VMEM(filterbank.shape, filterbank.dtype),
            pltpu.SMEM(shift_table.shape, shift_table.dtype),
            pltpu.SemaphoreType.DMA((channels // 16,)),
            pltpu.SemaphoreType.DMA,
            pltpu.VMEM((wide // LANES, channels * SUB, LANES), f32),
            pltpu.VMEM((16, SUB, wide), f32),
            pltpu.VMEM((8, 2, SUB, wide), f32),
            pltpu.VMEM((4, 4, SUB, wide), f32),
            pltpu.VMEM((2, 8, SUB, wide), f32),
            pltpu.VMEM((ROWS, SUB, wide), f32),
            pltpu.VMEM((ROWS, 2, LANES), f32),
            pltpu.VMEM((group, held, 2, LANES), f32),
            pltpu.VMEM((ROWS, 2, LANES), f32),
        ]
        + [pltpu.SemaphoreType.DMA((group,))] * 6
        + [pltpu.SemaphoreType.DMA],
        compiler_params=pltpu.CompilerParams(collective_id=0, has_side_effects=True),
    )(filterbank, shift_table)


def exchange_kernel(bits, stride, block, rows, row_send, row_recv, own_sem):
    group = 1 << bits
    held = ROWS // group
    me = lax.axis_index("chan")
    digit = (me // stride) % group
    mine = digit_bits(digit, bits)
    _, my_turn = partner(mine, 0)
    rounds = peer_rounds(bits)
    peers = {}
    for k in rounds:
        plain, turned = partner(mine, k)
        peers[k] = (me + (plain - digit) * stride, turned)
    barrier = enter([peers[k][0] for k in rounds])
    pl.semaphore_wait(barrier, len(rounds))
    there = rows.at[pl.ds(digit * held, held)]
    copies = {}
    for k in rounds:
        chan, turned = peers[k]
        copies[k] = remote(block.at[pl.ds(turned * held, held)], there, row_send, row_recv, k, chan)
        copies[k].start()
    own = pltpu.make_async_copy(block.at[pl.ds(my_turn * held, held)], there, own_sem)
    own.start()
    own.wait()
    for k in rounds:
        copies[k].wait()


def exchange(block, bits, stride, number):
    group = 1 << bits
    return pl.pallas_call(
        functools.partial(exchange_kernel, bits, stride),
        out_shape=jax.ShapeDtypeStruct(block.shape, block.dtype),
        in_specs=[pl.BlockSpec(memory_space=pltpu.VMEM)],
        out_specs=pl.BlockSpec(memory_space=pl.ANY),
        scratch_shapes=[pltpu.SemaphoreType.DMA((group,))] * 2 + [pltpu.SemaphoreType.DMA],
        compiler_params=pltpu.CompilerParams(
            collective_id=number, has_side_effects=True
        ),
    )(block)


def merge_rows(bits, merged, largest, block, correction, table, place, levels, keep, halves):
    group = 1 << bits
    held = ROWS // group
    wide = block.shape[-1]
    count = wide // LANES
    sub = lax.broadcasted_iota(jnp.int32, (SUB, LANES), 0)

    def put(level, row, tiles, is_upper):
        if level == bits:
            keep(row, tiles)
            return
        for m in range(count):
            levels[level][row, :, m * LANES : (m + 1) * LANES] = tiles[m]
            if is_upper and m * LANES < 2 * (merged * ROWS << level + 1):
                levels[level][row, :, wide + m * LANES : wide + (m + 1) * LANES] = next_sublane(tiles[m])

    def load(base):
        for c in range(ROWS // 2):
            tiles = []
            for m in range(count):
                w = slice(m * LANES, (m + 1) * LANES)
                tile = block[base + c, :, w]
                tiles.append(tile if correction is None else tile - correction[c % held, :, w])
            put(0, base + c, tiles, c // held % 2 == 1)

    def run(level, base, size):
        trials = held << level
        now = 2 * trials
        whole = merged * ROWS << level + 1
        source = levels[level]
        start = 2 * now * place
        at = start % wide // LANES
        pairs = [(q, i) for i in range(now) for q in range(size // now)]
        for first in range(0, size, 8):
            made = []
            for q, i in pairs[first : first + 8]:
                shift = table[whole - 1 + place * now + i]
                low = base + 2 * q * trials + i // 2
                high = low + trials
                tiles = [
                    source[high, :, pl.ds(pl.multiple_of((at + m) * LANES, LANES), LANES)]
                    for m in range(count + 1)
                ]
                moved = combine(tiles, shift & (LANES - 1))
                if largest >= wide:
                    up = jnp.minimum(start // wide, SUB)
                    moved = [
                        jnp.where(sub < SUB - up, pltpu.roll(tile, (SUB - up) & (SUB - 1), 0), 0.0)
                        for tile in moved
                    ]
                lower = [source[low, :, m * LANES : (m + 1) * LANES] for m in range(count)]
                made.append((base + q * now + i, plus(lower, moved), q % 2 == 1 or now == size))
            for row, tiles, is_upper in made:
                put(level + 1, row, tiles, is_upper)

    for base, ready in halves:
        ready()
        load(base)
        for level in range(bits - 1):
            run(level, base, ROWS // 2)
    run(bits - 1, 0, ROWS)


def stage_position(merged, bits):
    me = lax.axis_index("chan")
    known = merged.bit_length() - 1 + bits
    return partner(digit_bits(me, known), 0)[1]


def middle_kernel(bits, merged, largest, corrected, table_far, block, *rest):
    correction = rest[0] if corrected else None
    out, table, table_sem = rest[corrected : corrected + 3]
    levels = rest[corrected + 3 :]
    table_in = pltpu.make_async_copy(table_far, table, table_sem)
    table_in.start()

    def keep(row, tiles):
        for m in range(len(tiles)):
            out[row, :, m * LANES : (m + 1) * LANES] = tiles[m]

    place = stage_position(merged, bits)
    halves = [(0, table_in.wait), (ROWS // 2, lambda: None)]
    merge_rows(bits, merged, largest, block, correction, table, place, levels, keep, halves)


def back_kernel(bits, merged, largest, corrected, table_far, widths_far, block_far, *rest):
    dedispersed_far, peaks, flat, widths, widths_sem, table, table_sem = rest[corrected : corrected + 7]
    block, block_sem, dedispersed, dedispersed_sem, *levels = rest[corrected + 7 :]
    halves_in = []
    for n in range(2):
        part = pl.ds(n * (ROWS // 2), ROWS // 2)
        halves_in.append(pltpu.make_async_copy(block_far.at[part], block.at[part], block_sem.at[n]))
        halves_in[n].start()
    correction = None
    if corrected:
        correction, correction_sem, *levels = levels
        correction_in = pltpu.make_async_copy(rest[0], correction, correction_sem)
        correction_in.start()
    wide = block.shape[-1]
    length = wide * SUB
    table_in = pltpu.make_async_copy(table_far, table, table_sem)
    widths_in = pltpu.make_async_copy(widths_far, widths, widths_sem)
    table_in.start()
    widths_in.start()

    def keep(row, tiles):
        for m in range(len(tiles)):
            flat[m, row * SUB : (row + 1) * SUB, :] = tiles[m]

    place = stage_position(merged, bits)

    def first():
        halves_in[0].wait()
        if corrected:
            correction_in.wait()
        table_in.wait()

    halves = [(0, first), (ROWS // 2, halves_in[1].wait)]
    merge_rows(bits, merged, largest, block, correction, table, place, levels, keep, halves)
    dedispersed_out = pltpu.make_async_copy(dedispersed, dedispersed_far, dedispersed_sem)
    finish(length, flat, widths_in, widths, dedispersed, dedispersed_out, peaks)
    dedispersed_out.wait()


def finish(length, flat, widths_in, widths, dedispersed, dedispersed_out, peaks):
    wide = length // SUB
    series = [
        jnp.concatenate([flat[m, pl.ds(s, ROWS, stride=SUB), :] for m in range(wide // LANES)], axis=1)
        for s in range(SUB)
    ]
    summed = series[0]
    for part in series[1:]:
        summed = summed + part
    centre = jnp.sum(summed, axis=1, keepdims=True) * (1.0 / length)
    series = [part - centre for part in series]
    squared = jnp.square(series[0])
    for part in series[1:]:
        squared = squared + jnp.square(part)
    spread = jnp.sum(squared, axis=1, keepdims=True) * (1.0 / length)
    factor = lax.rsqrt(spread + epsilon)
    series = [part * factor for part in series]
    for s in range(SUB):
        dedispersed[:, s * wide : (s + 1) * wide] = series[s].astype(jnp.bfloat16)
    dedispersed_out.start()

    piece = 2 * LANES
    stacked = jnp.concatenate(
        [part[:, a : a + piece] for part in series for a in range(0, wide, piece)], axis=0
    )
    triangle = jnp.where(
        lax.broadcasted_iota(jnp.int32, (piece, piece + LANES), 0)
        <= lax.broadcasted_iota(jnp.int32, (piece, piece + LANES), 1),
        1.0,
        0.0,
    ).astype(jnp.bfloat16)
    rest_value = stacked
    inner = None
    for _ in range(3):
        top = rest_value.astype(jnp.bfloat16)
        rest_value = rest_value - top.astype(jnp.float32)
        product = jnp.dot(top, triangle, preferred_element_type=jnp.float32)
        inner = product if inner is None else inner + product
    offset = jnp.zeros((ROWS, LANES), jnp.float32)
    prefix = []
    for p in range(length // piece):
        one = inner[p * ROWS : (p + 1) * ROWS, :]
        prefix += [one[:, :LANES] + offset, one[:, LANES:piece] + offset]
        offset = offset + one[:, piece:]

    lane = lax.broadcasted_iota(jnp.int32, (ROWS, LANES), 1)
    diagonal = lane == lax.broadcasted_iota(jnp.int32, (ROWS, LANES), 0)
    zero = jnp.zeros((ROWS, LANES), jnp.float32)
    count = peaks.shape[0]
    widths_in.wait()
    for i in range(count):
        width = widths[i]
        whole, amount = divmod(1 << i, LANES)
        amount = width - whole * LANES
        keep = lane >= amount
        best = None
        before = zero
        for c in range(len(prefix)):
            source = c - whole
            now = pltpu.roll(prefix[source], amount, 1) if source >= 0 else zero
            box = prefix[c] - jnp.where(keep, now, before)
            before = now
            best = box if best is None else jnp.maximum(best, box)
        root = lax.rsqrt(jnp.full((ROWS, 1), width, jnp.int32).astype(jnp.float32))
        column = jnp.max(best, axis=1, keepdims=True) * root
        line = jnp.sum(jnp.where(diagonal, column, 0.0), axis=0, keepdims=True)
        peaks[i : i + 1, :] = line[:, :ROWS]


def merge(block, correction, shift_table, bits, merged, box_widths):
    wide = block.shape[-1]
    largest = 2 * ((merged * ROWS << bits) - 1) + 1
    corrected = correction is not None
    far = pl.BlockSpec(memory_space=pltpu.HBM)
    vmem = pl.BlockSpec(memory_space=pltpu.VMEM)
    levels = [pltpu.VMEM((ROWS, SUB, 2 * wide), jnp.float32)] * bits
    table = [pltpu.SMEM(shift_table.shape, shift_table.dtype), pltpu.SemaphoreType.DMA]
    params = pltpu.CompilerParams()
    data = (block, correction) if corrected else (block,)
    if box_widths is None:
        return pl.pallas_call(
            functools.partial(middle_kernel, bits, merged, largest, corrected),
            out_shape=jax.ShapeDtypeStruct(block.shape, jnp.float32),
            in_specs=[far] + [vmem] * len(data),
            out_specs=vmem,
            scratch_shapes=table + levels,
            compiler_params=params,
        )(shift_table, *data)
    widths = [pltpu.SMEM(box_widths.shape, box_widths.dtype), pltpu.SemaphoreType.DMA]
    staged = [
        pltpu.VMEM(block.shape, block.dtype),
        pltpu.SemaphoreType.DMA((2,)),
        pltpu.VMEM((ROWS, SUB * wide), jnp.bfloat16),
        pltpu.SemaphoreType.DMA,
    ]
    if corrected:
        staged += [pltpu.VMEM(correction.shape, correction.dtype), pltpu.SemaphoreType.DMA]
    return pl.pallas_call(
        functools.partial(back_kernel, bits, merged, largest, corrected),
        out_shape=(
            jax.ShapeDtypeStruct((ROWS, SUB * wide), jnp.bfloat16),
            jax.ShapeDtypeStruct((box_widths.shape[0], ROWS), jnp.float32),
        ),
        in_specs=[far] * (2 + len(data)),
        out_specs=(pl.BlockSpec(memory_space=pl.ANY), vmem),
        scratch_shapes=[pltpu.VMEM((wide // LANES, ROWS * SUB, LANES), jnp.float32)] + widths + table + staged + levels,
        compiler_params=params,
    )(shift_table, box_widths, *data)


def shards(filterbank, shift_table, box_widths):
    devices = lax.axis_size("chan")
    all_bits = devices.bit_length() - 1
    bits = min(GROUP_BITS, all_bits)
    rows, correction = front(filterbank, shift_table, bits, filterbank.shape[0] * devices)
    for bit in range(bits, all_bits):
        route = [(source, source ^ 1 << bit) for source in range(devices)]
        correction = correction + lax.ppermute(correction, "chan", route)
    done = 0
    while True:
        last = done + bits == all_bits
        result = merge(rows, correction, shift_table, bits, 1 << done, box_widths if last else None)
        if last:
            return result
        done += bits
        bits = min(GROUP_BITS, all_bits - done)
        rows = exchange(result, bits, 1 << done, done)
        correction = None


def solution(mesh):
    placed = (P(("beam", "chan"), None), P(), P())
    return jax.shard_map(
        shards,
        mesh=mesh,
        in_specs=placed,
        out_specs=(P(("beam", "chan"), None), P("beam", "chan")),
        check_vma=False,
    )
```
